128 devices in a mesh: dp: 32 (over y, z, core), ctx: 4 (over x).
Axes of the slice: x: 4, y: 4, z: 4, core: 2. Of those that a mesh axis runs over, the one named last changes fastest.
Arguments:
- tokens: bfloat16 [32, 1024, 4096], P('dp', 'ctx'), may hold values from -40.5 to 40.5
- doc_ids: int32 [32, 1024], P('dp', 'ctx'), may hold values from 0 to 5, never falling along the last dimension, each value on 1 to 512 neighbouring positions
- destinations: int32 [32], replicated, may hold values from 0 to 31, as said below
- norm_gain: float32 [4096], replicated, may hold values from 0.1 to 1.9
- w_query: bfloat16 [4096, 4096], P(None, 'ctx'), may hold values from -1 to 1
- w_key: bfloat16 [4096, 1024], P(None, 'ctx'), may hold values from -1 to 1
- w_value: bfloat16 [4096, 1024], P(None, 'ctx'), may hold values from -0.09375 to 0.09375
- w_out: bfloat16 [4096, 4096], P('ctx'), may hold values from -0.09375 to 0.09375
Outputs:
- attended: bfloat16 [32, 1024, 4096], P('dp', 'ctx')
- kv_cache: bfloat16 [32, 1024, 2048], P('dp', None, 'ctx')
The draws below stay inside these ranges and needn't reach their ends.
Inputs may be any that keep to these rules, and one draw needn't show every extreme that they name: `doc_ids`: within a packed row the document numbers never fall; a document covers 1 to 512 positions, and some document covers exactly 512. destinations is a permutation of the groups made by sections b = 0, 1, ... up to log2 32 - 1 in order: in section b the two groups whose indices differ only in bit b either exchange the rows they hold or keep them. So before section b a row with anchor g sits at the group whose bits below b are those of destinations[g] and whose other bits are those of g.
All inputs are finite; a program needn't handle non-finite values.
Results may differ from the reference program's by a relative error of at most 0.0083.
Values may be sent and summed in bfloat16 or wider, within the bound.
No kernel may reach another device: no remote copies, remote signals or barrier semaphores. Data moves between devices by JAX's collectives and lax.ppermute only.
A program may use at most 128 MiB of HBM per device.

```python
import math
import jax
import jax.numpy as jnp
import numpy as np
from jax import lax

D = 4096
H = 32
KVH = 8
HD = 128
BLK = 1024
DOCS = 6
N_DP = 32


def draw_tokens(key, part):
    key = jax.random.fold_in(key, 1)
    column_key, row_key, entry_key = jax.random.split(key, 3)
    column_scale = jnp.exp(jax.random.uniform(column_key, (D,), jnp.float32, math.log(0.3), math.log(3.0)))
    row_scale = jnp.exp(jax.random.uniform(row_key, (N_DP, BLK, 1), jnp.float32, math.log(0.3), math.log(3.0)))
    entries = jnp.clip(jax.random.normal(entry_key, (N_DP, BLK, D), jnp.float32), -4.5, 4.5)
    return (entries * column_scale * row_scale).astype(jnp.bfloat16)


def draw_w_key(key, part):
    key = jax.random.fold_in(key, 3)
    fresh = jax.random.normal(key, (D, KVH * HD), jnp.float32) / math.sqrt(D)
    return jnp.clip(fresh, -1.0, 1.0).astype(jnp.bfloat16)


def draw_w_query(key, part):
    key = jax.random.fold_in(key, 4)
    fresh = jax.random.normal(key, (D, H * HD), jnp.float32) / math.sqrt(D)
    return jnp.clip(fresh, -1.0, 1.0).astype(jnp.bfloat16)


def draw_destinations(key, part):
    key = jax.random.fold_in(key, 5)
    bit_count = N_DP.bit_length() - 1
    placed = jnp.arange(N_DP, dtype=jnp.int32)
    for bit in range(bit_count):
        section_key = jax.random.fold_in(key, bit)
        flag_key, forced_key = jax.random.split(section_key)
        flags = jax.random.randint(flag_key, (N_DP // 2,), 0, 2, jnp.int32)
        forced = jax.random.randint(forced_key, (), 0, N_DP // 2, jnp.int32)
        flags = flags.at[forced].set(1)
        low_mask = (1 << bit) - 1
        pair_index = jnp.right_shift(placed, bit + 1) * (1 << bit) + jnp.bitwise_and(placed, low_mask)
        placed = jnp.where(flags[pair_index] == 1, jnp.bitwise_xor(placed, 1 << bit), placed)
    return placed.astype(jnp.int32)


def steps_of(stream_key, dims, pieces, smallest, high):
    def one(dim, parts):
        heights = jax.random.uniform(jax.random.fold_in(jax.random.fold_in(stream_key, 6), dim), (parts,), jnp.float32, smallest / len(pieces), high / len(pieces))
        return jnp.repeat(jnp.exp(heights), dims[dim] // parts).reshape((-1,) + (1,) * (len(dims) - dim - 1))

    level = one(*pieces[0])
    for cut in pieces[1:]:
        level = level * one(*cut)
    return level


def length_profile(amount, total, most, lean):
    weights = [(1 << 20) // math.isqrt(rank ** lean) + 1 for rank in range(2, amount + 1)]
    rest, counts = total - most - (amount - 1), [1] * (amount - 1)
    while rest > 0:
        movable = [i for i in range(amount - 1) if counts[i] < most]
        pool, left = sum([weights[i] for i in movable]), rest
        for i in movable:
            more = min(most - counts[i], max(1, left * weights[i] // pool), rest)
            counts[i] = counts[i] + more
            rest = rest - more
    return np.array([most] + counts)


def ragged_sizes(key, amount, total, bound, lean):
    if amount == 2:
        one = jax.random.randint(key, (), max(1, total - bound), min(bound, total - 1) + 1)
        return jnp.stack([one, total - one])
    sizes = jnp.asarray(length_profile(amount, total, bound, lean), jnp.int32)
    twos = (amount - 1) // 2
    donor, sink = sizes[1:1 + 2 * twos:2], sizes[2:2 + 2 * twos:2]
    margin = jnp.minimum(donor - 1, bound - sink)
    shifted = jax.random.randint(jax.random.fold_in(key, 1), (twos,), 0, 1 << 20) % (margin + 1)
    sizes = sizes.at[1:1 + 2 * twos:2].set(donor - shifted).at[2:2 + 2 * twos:2].set(sink + shifted)
    return sizes[jax.random.permutation(jax.random.fold_in(key, 2), amount)]


def noise(rng, extent, width, limit, cuts=(), kind=jnp.bfloat16):
    values = jax.random.normal(rng, extent, jnp.float32) * width
    if len(cuts) > 0:
        values = steps_of(rng, extent, cuts, -0.22, 0.18) * values
    return jnp.clip(values, min=-limit, max=limit).astype(kind)


def setup_inputs(seed: int = 0) -> dict:
    keys = jax.random.split(jax.random.key(seed), 9)
    return {
        "tokens": draw_tokens(jax.random.fold_in(keys[8], 71), 0),
        "doc_ids": jax.vmap(lambda own: jnp.searchsorted(jnp.cumsum(ragged_sizes(own, DOCS, BLK, BLK // 2, 2)), jnp.arange(BLK), side="right"))(jax.random.split(keys[1], N_DP)).reshape((N_DP, BLK)).astype(jnp.int32),
        "destinations": draw_destinations(jax.random.fold_in(keys[8], 71), 0),
        "norm_gain": jnp.clip(1.0 + 0.18 * jax.random.normal(keys[3], (D,), jnp.float32), 0.1, 1.9),
        "w_query": draw_w_query(jax.random.fold_in(keys[8], 71), 0),
        "w_key": draw_w_key(jax.random.fold_in(keys[8], 71), 0),
        "w_value": noise(keys[6], (D, KVH * HD), D ** -0.5, 0.09375, ((1, 4),)),
        "w_out": noise(keys[7], (H * HD, D), (H * HD) ** -0.5, 0.09375, ((0, 4),)),
    }


def positions_of(doc_numbers):
    length = doc_numbers.shape[-1]
    row_index = jnp.arange(length, dtype=jnp.int32)
    same_doc = doc_numbers[..., :, None] == doc_numbers[..., None, :]
    doc_start = lax.optimization_barrier(jnp.min(jnp.where(same_doc, row_index, length), axis=-1))
    return (row_index - doc_start).astype(jnp.float32)

def rotate(columns, positions):
    half_dim = columns.shape[-1] // 2
    inverse = 500000.0 ** (-2.0 * jnp.arange(half_dim, dtype=jnp.float32) / columns.shape[-1])
    angles = positions[..., None, None] * inverse
    cosine = jnp.cos(angles)
    sine_part = jnp.sin(angles)
    first_half = columns[..., :half_dim]
    second_half = columns[..., half_dim:]
    return jnp.concatenate([first_half * cosine - second_half * sine_part, second_half * cosine + first_half * sine_part], axis=-1)

def reference(tokens, doc_ids, destinations, norm_gain, w_query, w_key, w_value, w_out):
    pack_count, length, model_width = tokens.shape
    head_count = w_query.shape[1] // HD
    kv_heads = w_key.shape[1] // HD
    group_size = head_count // kv_heads
    score_scale = 1.0 / math.sqrt(HD)
    flat_rows = tokens.reshape(-1, model_width).astype(jnp.float32)
    normed = (flat_rows * lax.rsqrt(lax.optimization_barrier(jnp.mean(flat_rows * flat_rows, axis=-1, keepdims=True)) + 1e-05) * norm_gain).astype(jnp.bfloat16)
    positions = positions_of(doc_ids)
    queries = jnp.dot(normed, w_query, preferred_element_type=jnp.float32).reshape(pack_count, length, head_count, HD)
    queries = rotate(queries, positions).astype(jnp.bfloat16)
    rotated_keys = jnp.dot(normed, w_key, preferred_element_type=jnp.float32).reshape(pack_count, length, kv_heads, HD)
    rotated_keys = rotate(rotated_keys, positions).astype(jnp.bfloat16)
    values = jnp.dot(normed, w_value, preferred_element_type=jnp.float32).astype(jnp.bfloat16).reshape(pack_count, length, kv_heads, HD)
    row_index = jnp.arange(length, dtype=jnp.int32)
    causal = row_index[None, :] <= row_index[:, None]

    def one_pack(inputs):
        pack_queries, pack_keys, pack_values, pack_ids = inputs
        grouped = pack_queries.astype(jnp.float32).reshape(length, kv_heads, group_size, HD)
        scores = jnp.einsum('ikgd,jkd->kgij', grouped, pack_keys.astype(jnp.float32)) * score_scale
        allowed = causal & (pack_ids[:, None] == pack_ids[None, :])
        scores = jnp.where(allowed, scores, -1e+30)
        row_max = lax.optimization_barrier(jnp.max(scores, axis=-1, keepdims=True))
        exp_scores = jnp.exp(scores - row_max)
        attn_weights = (exp_scores / lax.optimization_barrier(jnp.sum(exp_scores, axis=-1, keepdims=True))).astype(jnp.bfloat16)
        context = jnp.einsum('kgij,jkd->ikgd', attn_weights.astype(jnp.float32), pack_values.astype(jnp.float32))
        return context.astype(jnp.bfloat16).reshape(length, head_count * HD)
    context = lax.map(one_pack, (queries, rotated_keys, values, doc_ids))
    attended = jnp.dot(context.reshape(-1, head_count * HD), w_out, preferred_element_type=jnp.float32)
    attended = attended.astype(jnp.bfloat16).reshape(pack_count, length, model_width)
    kv_block = jnp.stack([rotated_keys, values], axis=3).reshape(pack_count, length, kv_heads * 2 * HD)
    kv_cache = jnp.zeros_like(kv_block).at[destinations.astype(jnp.int32)].set(kv_block)
    return (attended, kv_cache)
```

```python
import math

import jax
import jax.numpy as jnp
from jax import lax
from jax.sharding import PartitionSpec as P

HD = 128


def positions_of(doc_numbers):
    length = doc_numbers.shape[-1]
    row_index = jnp.arange(length, dtype=jnp.int32)
    same_doc = doc_numbers[..., :, None] == doc_numbers[..., None, :]
    doc_start = jnp.min(jnp.where(same_doc, row_index, length), axis=-1)
    return (row_index - doc_start).astype(jnp.float32)


def rotate(columns, positions):
    half_dim = columns.shape[-1] // 2
    inverse = 500000.0 ** (-2.0 * jnp.arange(half_dim, dtype=jnp.float32) / columns.shape[-1])
    angles = positions[..., None, None] * inverse
    cosine = jnp.cos(angles)
    sine_part = jnp.sin(angles)
    first_half = columns[..., :half_dim]
    second_half = columns[..., half_dim:]
    return jnp.concatenate(
        [
            first_half * cosine - second_half * sine_part,
            second_half * cosine + first_half * sine_part,
        ],
        axis=-1,
    )


def routed(block, destinations):
    groups = lax.axis_size("dp")
    anchors = jnp.arange(groups, dtype=jnp.int32)
    source = jnp.sum(jnp.where(destinations[None, :] == anchors[:, None], anchors[None, :], 0), axis=1)
    pieces = block.reshape(groups, block.shape[0] // groups, block.shape[1])
    scattered = lax.all_to_all(pieces, "dp", 0, 0, tiled=False)
    ordered = jnp.take(scattered, source, axis=0)
    return lax.all_to_all(ordered, "dp", 0, 0, tiled=False).reshape(block.shape)


def attention_layer(rows_local, ids_local, norm_gain, w_query, w_key, w_value, w_out):
    whole_rows, whole_ids = (
        lax.all_gather(rows_local[None], "ctx", axis=0, tiled=True),
        lax.all_gather(ids_local[None], "ctx", axis=0, tiled=True),
    )
    ctx_count, pack_count, shard_rows, model_width = whole_rows.shape
    length = ctx_count * shard_rows
    local_heads = w_query.shape[1] // HD
    local_kv = w_key.shape[1] // HD
    group_size = local_heads // local_kv
    score_scale = 1.0 / math.sqrt(HD)
    seq_rows = whole_rows.transpose(1, 0, 2, 3).reshape(pack_count * length, model_width)
    seq_ids = whole_ids.transpose(1, 0, 2).reshape(pack_count, length)
    flat_rows = seq_rows.astype(jnp.float32)
    normed = (
        flat_rows
        * lax.rsqrt(jnp.mean(flat_rows * flat_rows, axis=-1, keepdims=True) + 1e-05)
        * norm_gain
    ).astype(jnp.bfloat16)
    positions = positions_of(seq_ids)
    queries = jnp.dot(normed, w_query, preferred_element_type=jnp.float32).reshape(
        pack_count, length, local_heads, HD
    )
    queries = rotate(queries, positions).astype(jnp.bfloat16)
    queries = queries.reshape(pack_count, length, local_kv, group_size, HD)
    rotated_keys = jnp.dot(normed, w_key, preferred_element_type=jnp.float32).reshape(
        pack_count, length, local_kv, HD
    )
    rotated_keys = rotate(rotated_keys, positions).astype(jnp.bfloat16)
    values = jnp.dot(normed, w_value, preferred_element_type=jnp.float32).astype(jnp.bfloat16)
    values = values.reshape(pack_count, length, local_kv, HD)
    row_index = jnp.arange(length, dtype=jnp.int32)
    causal = row_index[None, :] <= row_index[:, None]
    allowed = (causal[None] & (seq_ids[:, :, None] == seq_ids[:, None, :]))[:, None]

    def one_head(inputs):
        head_queries, head_keys, head_values = inputs
        scores = (
            jnp.einsum(
                "nigd,njd->ngij", head_queries, head_keys, preferred_element_type=jnp.float32
            )
            * score_scale
        )
        scores = jnp.where(allowed, scores, -1e30)
        row_max = jnp.max(scores, axis=-1, keepdims=True)
        exp_scores = jnp.exp(scores - row_max)
        attn_weights = (exp_scores / jnp.sum(exp_scores, axis=-1, keepdims=True)).astype(
            jnp.bfloat16
        )
        context = jnp.einsum(
            "ngij,njd->nigd", attn_weights, head_values, preferred_element_type=jnp.float32
        )
        return context.astype(jnp.bfloat16)

    per_head = lax.map(
        one_head,
        (
            queries.transpose(2, 0, 1, 3, 4),
            rotated_keys.transpose(2, 0, 1, 3),
            values.transpose(2, 0, 1, 3),
        ),
    )
    context = per_head.transpose(1, 2, 0, 3, 4).reshape(
        pack_count, ctx_count, shard_rows, local_heads * HD
    )
    context = context.transpose(1, 0, 2, 3).reshape(
        ctx_count * pack_count * shard_rows, local_heads * HD
    )
    attended = lax.psum_scatter(
        jnp.dot(context, w_out, preferred_element_type=jnp.float32),
        "ctx",
        scatter_dimension=0,
        tiled=True,
    )
    attended = attended.astype(jnp.bfloat16).reshape(pack_count, shard_rows, model_width)
    kv_block = jnp.stack([rotated_keys, values], axis=3).reshape(
        pack_count, length, local_kv * 2 * HD
    )
    return (attended, kv_block)


def shards(tokens, doc_ids, destinations, norm_gain, w_query, w_key, w_value, w_out):
    attended, kv_block = attention_layer(
        tokens, doc_ids, norm_gain, w_query, w_key, w_value, w_out
    )
    return (attended, routed(kv_block[0], destinations)[None])


def solution(mesh):
    return jax.shard_map(
        shards,
        mesh=mesh,
        in_specs=(
            P("dp", "ctx", None),
            P("dp", "ctx"),
            P(),
            P(),
            P(None, "ctx"),
            P(None, "ctx"),
            P(None, "ctx"),
            P("ctx", None),
        ),
        out_specs=(P("dp", "ctx", None), P("dp", None, "ctx")),
        check_vma=False,
    )
```

```python
import functools
import math

import jax
import jax.numpy as jnp
from jax import lax
from jax.experimental import pallas as pl
from jax.experimental.pallas import tpu as pltpu
from jax.sharding import PartitionSpec as P

HD = 128
MIB = 1 << 20


def shifted(value, axis, by):
    count = lax.axis_size(axis)
    return lax.ppermute(value, axis, [(i, (i + by) % count) for i in range(count)])


def normalised(rows, norm_gain):
    wide = rows.astype(jnp.float32)
    scale = lax.rsqrt(jnp.mean(wide * wide, axis=-1, keepdims=True) + 1e-05)
    return (wide * scale * norm_gain).astype(jnp.bfloat16)


def rotary_tables(positions):
    half = HD // 2
    inverse = 500000.0 ** (-2.0 * jnp.arange(half, dtype=jnp.float32) / HD)
    angles = positions[:, None] * inverse
    cosine, sine = jnp.cos(angles), jnp.sin(angles)
    return (
        jnp.concatenate([cosine, cosine], axis=-1),
        jnp.concatenate([-sine, sine], axis=-1),
    )


def project_kernel(low_ref, high_ref, cos_ref, sin_ref, wq_ref, wk_ref, wv_ref, q_ref, kv_ref):
    step = pl.program_id(0)
    cosine, sine = cos_ref[...], sin_ref[...]

    def product(w_ref):
        rows = jnp.concatenate([low_ref[...], high_ref[...]], axis=0)
        return jnp.dot(rows, w_ref[...], preferred_element_type=jnp.float32)

    def turned(columns):
        heads = [columns[:, i : i + HD] for i in range(0, columns.shape[1], HD)]
        return [h * cosine + pltpu.roll(h, HD // 2, 1) * sine for h in heads]

    @pl.when(step == 0)
    def _():
        for head, column in enumerate(turned(product(wk_ref))):
            kv_ref[head, :, :HD] = column.astype(kv_ref.dtype)

    @pl.when(step == 1)
    def _():
        values = product(wv_ref)
        for head in range(values.shape[1] // HD):
            kv_ref[head, :, HD:] = values[:, head * HD : (head + 1) * HD].astype(kv_ref.dtype)

    @pl.when(step >= 2)
    def _():
        for head, column in enumerate(turned(product(wq_ref))):
            q_ref[:, head * HD : (head + 1) * HD] = column.astype(q_ref.dtype)


def project(low, high, tables, w_query, w_key, w_value):
    rows, width = 2 * low.shape[0], low.shape[1]
    queries, keys = w_query.shape[1], w_key.shape[1]
    tile = 256
    whole = lambda shape: pl.BlockSpec(shape, lambda j: (0, 0))
    return pl.pallas_call(
        project_kernel,
        grid=(2 + queries // tile,),
        in_specs=[
            whole(low.shape),
            whole(high.shape),
            whole((rows, HD)),
            whole((rows, HD)),
            pl.BlockSpec((width, tile), lambda j: (0, jnp.maximum(j - 2, 0))),
            whole((width, keys)),
            whole((width, keys)),
        ],
        out_specs=[
            pl.BlockSpec((rows, tile), lambda j: (0, jnp.maximum(j - 2, 0))),
            pl.BlockSpec((keys // HD, rows, 2 * HD), lambda j: (0, 0, 0)),
        ],
        out_shape=[
            jax.ShapeDtypeStruct((rows, queries), jnp.bfloat16),
            jax.ShapeDtypeStruct((keys // HD, rows, 2 * HD), jnp.bfloat16),
        ],
        compiler_params=pltpu.CompilerParams(vmem_limit_bytes=28 * MIB),
        cost_estimate=pl.CostEstimate(
            flops=2 * rows * width * (queries + 2 * keys),
            bytes_accessed=2 * width * (queries + 2 * keys + rows),
            transcendentals=0,
        ),
        name="project",
    )(low, high, *tables, w_query, w_key, w_value)


def attend_kernel(info_ref, start_ref, q_ref, far_ref, near_ref, own_ref, out_ref):
    blocks, base = info_ref[0], info_ref[1]
    rows = q_ref.shape[0]
    kv_heads = own_ref.shape[0]
    group = q_ref.shape[1] // (kv_heads * HD)
    factor = math.log2(math.e) / math.sqrt(HD)

    def run(refs):
        count = len(refs) * rows
        column = lax.broadcasted_iota(jnp.int32, (rows, count), 1) + (base + rows - count)
        line = lax.broadcasted_iota(jnp.int32, (rows, count), 0) + base
        allowed = (column >= start_ref[...]) & (column <= line)
        for head in range(kv_heads):
            keys = jnp.concatenate([r[head, :, :HD] for r in refs], axis=0)
            values = jnp.concatenate([r[head, :, HD:] for r in refs], axis=0)
            for member in range(group):
                place = (head * group + member) * HD
                scores = lax.dot_general(
                    q_ref[:, place : place + HD],
                    keys,
                    (((1,), (1,)), ((), ())),
                    preferred_element_type=jnp.float32,
                )
                scores = jnp.where(allowed, scores, -1e30)
                most = jnp.max(scores, axis=-1, keepdims=True)
                weights = jnp.exp2((scores - most) * factor)
                total = jnp.sum(weights, axis=-1, keepdims=True)
                context = jnp.dot(
                    weights.astype(jnp.bfloat16), values, preferred_element_type=jnp.float32
                )
                out_ref[:, place : place + HD] = (context / total).astype(out_ref.dtype)

    @pl.when(blocks == 1)
    def _():
        run([own_ref])

    @pl.when(blocks == 2)
    def _():
        run([near_ref, own_ref])

    @pl.when(blocks == 3)
    def _():
        run([far_ref, near_ref, own_ref])


def attend(info, starts, queries, far, near, own):
    rows, width = queries.shape
    vmem = pl.BlockSpec(memory_space=pltpu.VMEM)
    return pl.pallas_call(
        attend_kernel,
        in_specs=[pl.BlockSpec(memory_space=pltpu.SMEM)] + [vmem] * 5,
        out_specs=vmem,
        out_shape=jax.ShapeDtypeStruct(queries.shape, jnp.bfloat16),
        compiler_params=pltpu.CompilerParams(vmem_limit_bytes=28 * MIB),
        cost_estimate=pl.CostEstimate(
            flops=4 * rows * 3 * rows * width,
            bytes_accessed=2 * (2 * rows * width + 3 * own.size),
            transcendentals=rows * 3 * rows * width // HD,
        ),
        name="attend",
    )(info, starts, queries, far, near, own)


def out_kernel(count, has_sum, *refs):
    out_ref = refs[-1]
    total = refs[2 * count][...] if has_sum else None
    for i in range(count):
        w_ref = refs[count + i]
        block = w_ref[0] if len(w_ref.shape) == 3 else w_ref[...]
        term = jnp.dot(refs[i][...], block, preferred_element_type=jnp.float32)
        total = term if total is None else total + term
    out_ref[...] = total.astype(out_ref.dtype)


def out_terms(contexts, weights, partial, dtype):
    rows, depth = contexts[0].shape
    width = weights[0][0].shape[-1]
    tile = 512
    in_specs = [pl.BlockSpec((rows, depth), lambda j: (0, 0)) for _ in contexts]
    for array, index in weights:
        if index is None:
            in_specs.append(pl.BlockSpec((depth, tile), lambda j: (0, j)))
        else:
            in_specs.append(
                pl.BlockSpec((1, depth, tile), functools.partial(lambda i, j: (i, 0, j), index))
            )
    operands = list(contexts) + [array for array, _ in weights]
    if partial is not None:
        in_specs.append(pl.BlockSpec((rows, tile), lambda j: (0, j)))
        operands.append(partial)
    return pl.pallas_call(
        functools.partial(out_kernel, len(contexts), partial is not None),
        grid=(width // tile,),
        in_specs=in_specs,
        out_specs=pl.BlockSpec((rows, tile), lambda j: (0, j)),
        out_shape=jax.ShapeDtypeStruct((rows, width), dtype),
        compiler_params=pltpu.CompilerParams(vmem_limit_bytes=24 * MIB),
        cost_estimate=pl.CostEstimate(
            flops=2 * len(contexts) * rows * depth * width,
            bytes_accessed=2 * len(contexts) * depth * width,
            transcendentals=0,
        ),
        name="out_terms",
    )(*operands)


def reorder_kernel(source_ref, in_ref, out_ref):
    def one(i, carry):
        out_ref[i] = in_ref[source_ref[i]]
        return carry

    lax.fori_loop(0, in_ref.shape[0], one, 0)


def routed(blocks, source):
    groups = lax.axis_size("dp")
    pieces = [b.reshape(groups, -1, b.shape[-1]) for b in blocks]
    depth = pieces[0].shape[1]
    pieces = pieces[0] if len(pieces) == 1 else jnp.concatenate(pieces, axis=1)
    scattered = lax.all_to_all(pieces, "dp", 0, 0, tiled=False)
    vmem = pl.BlockSpec(memory_space=pltpu.VMEM)
    ordered = pl.pallas_call(
        reorder_kernel,
        in_specs=[pl.BlockSpec(memory_space=pltpu.SMEM), vmem],
        out_specs=vmem,
        out_shape=jax.ShapeDtypeStruct(pieces.shape, pieces.dtype),
        name="reorder",
    )(source, scattered)
    delivered = lax.all_to_all(ordered, "dp", 0, 0, tiled=False)
    return [
        delivered[:, i * depth : (i + 1) * depth].reshape(b.shape) for i, b in enumerate(blocks)
    ]


def shards(tokens, doc_ids, destinations, norm_gain, w_query, w_key, w_value, w_out):
    quarters = lax.axis_size("ctx")
    groups = lax.axis_size("dp")
    place = lax.axis_index("ctx")
    row = lax.axis_index("dp")
    rows = tokens.shape[1]
    half = rows // 2

    ids = [doc_ids[0]] + [shifted(doc_ids[0], "ctx", -e) for e in range(1, quarters)]

    share = w_out.shape[0] // groups
    mine = lax.dynamic_slice_in_dim(w_out, row * share, share, 0)
    shares = jnp.stack([shifted(mine, "ctx", e) for e in range(1, quarters)])
    others = lax.all_gather(shares, "dp", axis=1, tiled=True)

    normed = normalised(tokens[0], norm_gain)
    low, high = normed[:half], normed[half:]
    before_low, after_high = shifted(low, "ctx", 1), shifted(high, "ctx", -1)
    before_high, after_low = shifted(high, "ctx", 1), shifted(low, "ctx", -1)
    far_low, far_high = shifted(before_low, "ctx", 1), shifted(after_high, "ctx", -1)
    arrived = [(low, high), (after_low, after_high), (far_low, far_high), (before_low, before_high)]

    bases = [(place + e) % quarters * rows for e in range(quarters)]
    steps = jnp.arange(rows, dtype=jnp.int32)
    row_index = jnp.concatenate([b + steps for b in bases])
    row_ids = jnp.concatenate(ids)
    first = jnp.min(
        jnp.where(row_ids[:, None] == row_ids[None, :], row_index[None, :], quarters * rows), axis=-1
    )
    cosine, sine = rotary_tables((row_index - first).astype(jnp.float32))
    starts = [first[e * rows : (e + 1) * rows] for e in range(quarters)]
    infos = []
    for e in range(quarters):
        least = starts[e][0]
        count = 1 + (least < bases[e]).astype(jnp.int32) + (least < bases[e] - rows).astype(jnp.int32)
        infos.append(jnp.stack([count, bases[e]]))

    queries, kv = [None] * quarters, [None] * quarters
    for e in (0, 1, 3, 2):
        here = slice(e * rows, (e + 1) * rows)
        queries[e], kv[e] = project(
            *arrived[e], (cosine[here], sine[here]), w_query, w_key, w_value
        )

    contexts = [
        attend(infos[e], starts[e][:, None], queries[e], kv[e - 2], kv[e - 1], kv[e])
        for e in range(quarters)
    ]
    received = [contexts[0]] + [shifted(contexts[e], "ctx", e) for e in (1, 2, 3)]
    partial = out_terms([received[0]], [(w_out, None)], None, jnp.float32)
    partial = out_terms([received[2]], [(others, 1)], partial, jnp.float32)
    attended = out_terms(
        [received[1], received[3]], [(others, 0), (others, 2)], partial, jnp.bfloat16
    )

    anchors = jnp.arange(groups, dtype=jnp.int32)
    source = jnp.sum(jnp.where(destinations[None, :] == anchors[:, None], anchors[None, :], 0), axis=1)
    cache = [None] * quarters
    cache[0], cache[1], cache[3] = routed([kv[0], kv[1], kv[3]], source)
    (cache[2],) = routed([kv[2]], source)
    ordered = jnp.stack(cache).transpose(0, 2, 1, 3).reshape(quarters, rows, -1)
    kv_cache = jnp.roll(ordered, place, axis=0).reshape(quarters * rows, -1)
    return attended[None], kv_cache[None]


def solution(mesh):
    return jax.shard_map(
        shards,
        mesh=mesh,
        in_specs=(
            P("dp", "ctx", None),
            P("dp", "ctx"),
            P(),
            P(),
            P(None, "ctx"),
            P(None, "ctx"),
            P(None, "ctx"),
            P("ctx", None),
        ),
        out_specs=(P("dp", "ctx", None), P("dp", None, "ctx")),
        check_vma=False,
    )
```

```python
import functools
import math

import jax
import jax.numpy as jnp
from jax import lax
from jax.experimental import pallas as pl
from jax.experimental.pallas import tpu as pltpu
from jax.sharding import PartitionSpec as P

HD = 128
VMEM_LIMIT = 60 << 20
PROJECT_WEIGHT = 1
LAST_WEIGHT = 60
ATTEND_WEIGHT = 0


def shifted(value, axis, by):
    count = lax.axis_size(axis)
    return lax.ppermute(value, axis, [(i, (i + by) % count) for i in range(count)])


def normalised(rows, norm_gain):
    wide = rows.astype(jnp.float32)
    scale = lax.rsqrt(jnp.mean(wide * wide, axis=-1, keepdims=True) + 1e-05)
    return (wide * scale * norm_gain).astype(jnp.bfloat16)


def rotary_tables(positions):
    half = HD // 2
    inverse = 500000.0 ** (-2.0 * jnp.arange(half, dtype=jnp.float32) / HD)
    angles = positions[:, None] * inverse
    cosine, sine = jnp.cos(angles), jnp.sin(angles)
    return (
        jnp.concatenate([cosine, cosine], axis=-1),
        jnp.concatenate([-sine, sine], axis=-1),
    )


def project_kernel(plan, *refs):
    rows_ref, held, row_sems, sems = refs[-4:]
    parts = row_sems.shape[0]
    half_refs, refs = refs[:parts], refs[parts:]
    cos_ref, sin_ref, wq_ref, wk_ref, wv_ref = refs[:5]
    if plan is None:
        (out_ref,) = refs[5:6]
    else:
        info_ref, first_ref, own_ref, near_ref = refs[5:9]
        out_ref, pieces_ref, context_ref = refs[9:12]
    half = half_refs[0].shape[0]
    count, _, tile = held.shape
    wide = count - 2

    def source(i):
        if i < 2:
            return (wk_ref, wv_ref)[i]
        return wq_ref.at[:, pl.ds((i - 2) * tile, tile)]

    def start(i):
        pltpu.make_async_copy(source(i), held.at[i], sems.at[i]).start()

    moves = [
        pltpu.make_async_copy(ref, rows_ref.at[pl.ds(i * half, half)], row_sems.at[i])
        for i, ref in enumerate(half_refs)
    ]
    for move in moves:
        move.start()
    start(0)
    start(1)
    for move in moves:
        move.wait()

    def one(i, carry):
        pltpu.make_async_copy(wk_ref, held.at[i], sems.at[i]).wait()
        for k in range(2, count):
            pl.when(i == k - 2)(functools.partial(start, k))
        made = jnp.dot(rows_ref[...], held[i], preferred_element_type=jnp.float32)
        cosine = jnp.where(i == 1, 1.0, cos_ref[...])
        sine = jnp.where(i == 1, 0.0, sin_ref[...])
        slot = jnp.where(i < 2, i + wide, i - 2)
        for at in range(0, tile, HD):
            part = made[:, at : at + HD]
            part = part * cosine + pltpu.roll(part, HD // 2, 1) * sine
            out_ref[slot, :, at : at + HD] = part.astype(out_ref.dtype)
        return carry

    lax.fori_loop(0, count, one, 0)
    if plan is None:
        return
    rows = 2 * half
    kv_refs = [
        own_ref,
        near_ref.at[:, pl.ds(0, rows)],
        near_ref.at[:, pl.ds(rows, rows)],
        out_ref.at[pl.ds(wide, 2)],
    ]
    for kind in (0, 1):
        for slot, kv_ref in enumerate(kv_refs):
            pieces_ref[kind * 16 : (kind + 1) * 16, slot * 16 : (slot + 1) * 16] = kv_ref[
                kind
            ].reshape(16, 16, tile)

    def store(head, block):
        context_ref[:, head * HD : (head + 1) * HD] = block

    attend_quarter(info_ref, first_ref, kv_refs, {plan[1][0][0]: out_ref}, *plan, store)


def project(lot, arrived, tables, w_query, w_key, w_value, earlier=None):
    rows, width = len(arrived) * arrived[0].shape[0], arrived[0].shape[1]
    tile = w_key.shape[1]
    count = 2 + w_query.shape[1] // tile
    anywhere = pl.BlockSpec(memory_space=pl.ANY)
    table = pl.BlockSpec((pl.Element(rows), pl.Element(HD)), lambda i: (lot, 0))
    whole = lambda shape: pl.BlockSpec(shape, lambda i: (0,) * len(shape))
    operands = [*arrived, *tables, w_query, w_key, w_value]
    in_specs = [anywhere] * len(arrived) + [table] * 2 + [anywhere] * 3
    shapes = [(count, rows, tile)]
    plan, weight = None, PROJECT_WEIGHT
    if earlier is not None:
        info, first_wide, made, plan = earlier
        operands += [info, first_wide, *made]
        in_specs += [pl.BlockSpec(memory_space=pltpu.SMEM), whole(first_wide.shape)]
        in_specs += [
            pl.BlockSpec((2, m.shape[1], tile), lambda i: (count // 2 - 1, 0, 0)) for m in made
        ]
        shapes += [(32, 64, tile), (rows, (count - 2) * tile)]
        weight = LAST_WEIGHT
    return pl.pallas_call(
        functools.partial(project_kernel, plan),
        grid=(1,),
        in_specs=in_specs,
        out_specs=[whole(shape) for shape in shapes],
        out_shape=[jax.ShapeDtypeStruct(shape, jnp.bfloat16) for shape in shapes],
        scratch_shapes=[
            pltpu.VMEM((rows, width), jnp.bfloat16),
            pltpu.VMEM((count, width, tile), jnp.bfloat16),
            pltpu.SemaphoreType.DMA((len(arrived),)),
            pltpu.SemaphoreType.DMA((count,)),
        ],
        compiler_params=pltpu.CompilerParams(vmem_limit_bytes=VMEM_LIMIT),
        cost_estimate=pl.CostEstimate(
            flops=weight * 2 * rows * width * tile * count,
            bytes_accessed=2 * width * (tile * count + rows),
            transcendentals=0,
        ),
        name="project" if earlier is None else "project_attend",
    )(*operands)


def attend_quarter(info_ref, first_ref, kv_refs, q_refs, slots, q_slots, store):
    blocks, base = info_ref[0], info_ref[1]
    half = first_ref.shape[0] // 8
    rows = 2 * half
    factor = math.log2(math.e) / math.sqrt(HD)
    first = jnp.concatenate(
        [first_ref[lot * rows + at : lot * rows + at + half, :1] for lot, at in q_slots], axis=0
    )

    def run(used):
        count = used * rows
        column = lax.broadcasted_iota(jnp.int32, (rows, count), 1) + (base + rows - count)
        line = lax.broadcasted_iota(jnp.int32, (rows, count), 0) + base
        bias = jnp.where((column >= first) & (column <= line), 0.0, -1e30)
        ones = jnp.ones((count, HD), jnp.bfloat16)
        pieces = slots[2 * (3 - used) :]
        for kv_head in range(2):
            place = slice(kv_head * HD, (kv_head + 1) * HD)
            keys = jnp.concatenate([kv_refs[a][0, at : at + half, place] for a, at in pieces], axis=0)
            values = jnp.concatenate(
                [kv_refs[a][1, at : at + half, place] for a, at in pieces], axis=0
            )
            values = jnp.concatenate([values, ones], axis=1)
            for head in range(4 * kv_head, 4 * kv_head + 4):
                within = slice(head % 2 * HD, (head % 2 + 1) * HD)
                queries = jnp.concatenate(
                    [q_refs[a][head // 2, at : at + half, within] for a, at in q_slots], axis=0
                )
                scores = lax.dot_general(
                    queries, keys, (((1,), (1,)), ((), ())), preferred_element_type=jnp.float32
                )
                scores = scores + bias
                most = jnp.max(scores, axis=-1, keepdims=True)
                weights = jnp.exp2((scores - most) * factor).astype(jnp.bfloat16)
                summed = jnp.dot(weights, values, preferred_element_type=jnp.float32)
                store(head, (summed[:, :HD] / summed[:, HD:]).astype(jnp.bfloat16))

    for used in (1, 2, 3):
        pl.when(blocks == used)(functools.partial(run, used))


def attend_kernel(plan, lots, with_own, *refs):
    quarters = len(plan)
    info_refs, first_ref = refs[:quarters], refs[quarters]
    own_ref, near_ref, far_ref = refs[quarters + 1 : quarters + 4]
    rows = own_ref.shape[1]
    kv_refs = [own_ref, near_ref.at[:, pl.ds(0, rows)], near_ref.at[:, pl.ds(rows, rows)], far_ref]
    refs = refs[quarters + 4 :]
    q_refs = dict(zip(lots, refs))
    refs = refs[len(lots) :]
    if with_own:
        w_ref, out_ref, context, held, sems = refs
        tile = held.shape[2]
        copies = [
            pltpu.make_async_copy(w_ref.at[:, pl.ds(i * tile, tile)], held.at[i], sems.at[i])
            for i in range(held.shape[0])
        ]
        for copy in copies:
            copy.start()
        out_refs = [context]
    else:
        out_refs = refs[:quarters]
    for info_ref, out_ref_e, (slots, q_slots) in zip(info_refs, out_refs, plan):

        def store(head, block, out_ref_e=out_ref_e):
            out_ref_e[:, head * HD : (head + 1) * HD] = block

        attend_quarter(info_ref, first_ref, kv_refs, q_refs, slots, q_slots, store)
    if with_own:
        for i, copy in enumerate(copies):
            copy.wait()
            out_ref[:, i * tile : (i + 1) * tile] = jnp.dot(
                context[...], held[i], preferred_element_type=jnp.float32
            )


def attend(infos, first_wide, made, plan, w_out=None):
    count, rows, tile = made[0].shape
    width = (count - 2) * tile
    lots = sorted({a for _, q_slots in plan for a, _ in q_slots})
    spots = [((0, 0), (1, 0), (1, 1), (2, 0))[lot] for lot in lots]
    smem = pl.BlockSpec(memory_space=pltpu.SMEM)
    whole = lambda shape: pl.BlockSpec(shape, lambda i: (0,) * len(shape))
    in_specs = (
        [smem] * len(plan)
        + [whole(first_wide.shape)]
        + [pl.BlockSpec((2, m.shape[1], tile), lambda i: (count // 2 - 1, 0, 0)) for m in made]
        + [
            pl.BlockSpec((count - 2, rows, tile), functools.partial(lambda n, i: (0, n, 0), spot))
            for _, spot in spots
        ]
    )
    operands = [*infos, first_wide, *made, *[made[a] for a, _ in spots]]
    scratch = []
    if w_out is None:
        shapes = [jax.ShapeDtypeStruct((rows, width), jnp.bfloat16)] * len(plan)
    else:
        in_specs.append(pl.BlockSpec(memory_space=pl.ANY))
        operands.append(w_out)
        shapes = [jax.ShapeDtypeStruct((rows, w_out.shape[1]), jnp.float32)]
        scratch = [
            pltpu.VMEM((rows, width), jnp.bfloat16),
            pltpu.VMEM((4, width, w_out.shape[1] // 4), jnp.bfloat16),
            pltpu.SemaphoreType.DMA((4,)),
        ]
    return pl.pallas_call(
        functools.partial(attend_kernel, plan, lots, w_out is not None),
        grid=(1,),
        in_specs=in_specs,
        out_specs=[whole(shape.shape) for shape in shapes],
        out_shape=shapes,
        scratch_shapes=scratch,
        compiler_params=pltpu.CompilerParams(vmem_limit_bytes=VMEM_LIMIT),
        cost_estimate=pl.CostEstimate(
            flops=ATTEND_WEIGHT * 12 * len(plan) * rows * rows * width,
            bytes_accessed=2 * (2 * rows * width + 3 * made[0].size),
            transcendentals=0,
        ),
        name="attend",
    )(*operands)


def others_kernel(order, *refs):
    count = len(order)
    context_refs = refs[:count]
    w_ref, partial_ref, out_ref, held, sums, stacked, sems, sum_sems, context_sems = refs[count:]
    slots, _, tile = held.shape
    depth = w_ref.shape[1]
    steps = out_ref.shape[1] // tile

    def copies(step, slot):
        at = pl.multiple_of(step * tile, tile)
        return [
            pltpu.make_async_copy(
                w_ref.at[index, :, pl.ds(at, tile)],
                held.at[slot, pl.ds(i * depth, depth)],
                sems.at[slot, i],
            )
            for i, index in enumerate(order)
        ] + [
            pltpu.make_async_copy(
                partial_ref.at[:, pl.ds(at, tile)], sums.at[slot], sum_sems.at[slot]
            )
        ]

    gathers = [
        pltpu.make_async_copy(
            ref, stacked.at[:, pl.ds(i * depth, depth)], context_sems.at[i]
        )
        for i, ref in enumerate(context_refs)
    ]
    for gather in gathers:
        gather.start()
    for step in range(slots - 1):
        for copy in copies(step, step):
            copy.start()
    for gather in gathers:
        gather.wait()

    def one(step, carry):
        slot = lax.rem(step, slots)
        for copy in copies(step, slot):
            copy.wait()

        @pl.when(step + slots - 1 < steps)
        def _():
            for copy in copies(step + slots - 1, lax.rem(step + slots - 1, slots)):
                copy.start()

        total = sums[slot] + jnp.dot(
            stacked[...], held[slot], preferred_element_type=jnp.float32
        )
        out_ref[:, pl.ds(pl.multiple_of(step * tile, tile), tile)] = total.astype(out_ref.dtype)
        return carry

    lax.fori_loop(0, steps, one, 0)


def other_terms(contexts, order, others, partial):
    rows, depth = contexts[0].shape
    width = others.shape[-1]
    tile, slots, count = 512, 3, len(contexts)
    anywhere = pl.BlockSpec(memory_space=pl.ANY)
    return pl.pallas_call(
        functools.partial(others_kernel, order),
        grid=(1,),
        in_specs=[anywhere] * (count + 2),
        out_specs=pl.BlockSpec((rows, width), lambda i: (0, 0)),
        out_shape=jax.ShapeDtypeStruct((rows, width), jnp.bfloat16),
        scratch_shapes=[
            pltpu.VMEM((slots, count * depth, tile), jnp.bfloat16),
            pltpu.VMEM((slots, rows, tile), jnp.float32),
            pltpu.VMEM((rows, count * depth), jnp.bfloat16),
            pltpu.SemaphoreType.DMA((slots, count)),
            pltpu.SemaphoreType.DMA((slots,)),
            pltpu.SemaphoreType.DMA((count,)),
        ],
        compiler_params=pltpu.CompilerParams(vmem_limit_bytes=VMEM_LIMIT),
        cost_estimate=pl.CostEstimate(
            flops=2 * count * rows * depth * width,
            bytes_accessed=2 * count * depth * width,
            transcendentals=0,
        ),
        name="other_terms",
    )(*contexts, others, partial)


def reorder_kernel(source_ref, in_ref, out_ref):
    def one(i, carry):
        out_ref[i] = in_ref[source_ref[i]]
        return carry

    lax.fori_loop(0, in_ref.shape[0], one, 0)


def routed(pieces, source, after):
    scattered = lax.all_to_all(pieces, "dp", 0, 0, tiled=False)
    scattered, after = lax.optimization_barrier((scattered, after))
    whole = pl.BlockSpec(pieces.shape, lambda i: (0, 0, 0))
    ordered = pl.pallas_call(
        reorder_kernel,
        grid=(1,),
        in_specs=[pl.BlockSpec(memory_space=pltpu.SMEM), whole],
        out_specs=whole,
        out_shape=jax.ShapeDtypeStruct(pieces.shape, pieces.dtype),
        name="reorder",
    )(source, scattered)
    return lax.all_to_all(ordered, "dp", 0, 0, tiled=False), after


def assemble_kernel(spots, place_ref, pieces_ref, out_ref):
    quarters = len(spots) // 2
    rows = out_ref.shape[0] // quarters
    half = rows // 2
    for quarter in range(quarters):
        base = pl.multiple_of(lax.rem(place_ref[0] + quarter, quarters) * rows, rows)
        for which in (0, 1):
            slot, at = spots[2 * quarter + which]
            for kind in range(2):
                block = pieces_ref[
                    kind * 16 + at // 16 : kind * 16 + (at + half) // 16,
                    slot * 16 : (slot + 1) * 16,
                ].reshape(half, 2 * HD)
                for head in range(2):
                    to = (2 * head + kind) * HD
                    out_ref[pl.ds(base + which * half, half), to : to + HD] = block[
                        :, head * HD : (head + 1) * HD
                    ]


def assemble(spots, place, pieces, shape):
    whole = lambda shape: pl.BlockSpec(shape, lambda i: (0,) * len(shape))
    return pl.pallas_call(
        functools.partial(assemble_kernel, spots),
        grid=(1,),
        in_specs=[pl.BlockSpec(memory_space=pltpu.SMEM), whole(pieces.shape)],
        out_specs=whole(shape),
        out_shape=jax.ShapeDtypeStruct(shape, pieces.dtype),
        name="assemble",
    )(jnp.reshape(place, (1,)).astype(jnp.int32), pieces)


def shards(tokens, doc_ids, destinations, norm_gain, w_query, w_key, w_value, w_out):
    quarters = lax.axis_size("ctx")
    groups = lax.axis_size("dp")
    place = lax.axis_index("ctx")
    row = lax.axis_index("dp")
    rows = tokens.shape[1]
    half = rows // 2

    ids = [doc_ids[0]] + [shifted(doc_ids[0], "ctx", -e) for e in range(1, quarters)]

    share = w_out.shape[0] // groups
    mine = lax.dynamic_slice_in_dim(w_out, row * share, share, 0)
    shares = jnp.stack([shifted(mine, "ctx", e) for e in range(1, quarters)])

    normed = normalised(tokens[0], norm_gain)
    low, high = normed[:half], normed[half:]
    halves = [((0, 0), (0, 1)), ((1, 1), (3, 0)), ((1, 0), (3, 1)), ((2, 0), (2, 1))]
    where = {h: (i, j * half) for i, pair in enumerate(halves) for j, h in enumerate(pair)}

    bases = [(place + e) % quarters * rows for e in range(quarters)]
    steps = jnp.arange(half, dtype=jnp.int32)
    order = [h for pair in halves for h in pair]
    row_index = jnp.concatenate([bases[q] + (h * half + steps) for q, h in order])
    row_ids = jnp.concatenate([ids[q][h * half : (h + 1) * half] for q, h in order])
    first = jnp.min(
        jnp.where(row_ids[:, None] == row_ids[None, :], row_index[None, :], quarters * rows), axis=-1
    )
    cosine, sine = rotary_tables((row_index - first).astype(jnp.float32))
    first_wide = jnp.broadcast_to(first[:, None], (first.shape[0], HD))
    infos = []
    for e in range(quarters):
        lot, at = where[(e, 0)]
        least = first[lot * rows + at]
        count = 1 + (least < bases[e]).astype(jnp.int32) + (least < bases[e] - rows).astype(jnp.int32)
        infos.append(jnp.stack([count, bases[e]]))
    cosine, sine, first_wide, infos = lax.optimization_barrier((cosine, sine, first_wide, infos))

    before_low, after_high = shifted(low, "ctx", 1), shifted(high, "ctx", -1)
    then_low, then_high, _ = lax.optimization_barrier((low, high, first))
    before_high, after_low = shifted(then_high, "ctx", 1), shifted(then_low, "ctx", -1)
    far_low, far_high = shifted(before_low, "ctx", 1), shifted(after_high, "ctx", -1)
    low, high, shares = lax.optimization_barrier((low, high, shares))
    others = lax.all_gather(shares, "dp", axis=1, tiled=True)
    lots = [(low, high), (after_high, before_low), (after_low, before_high), (far_low, far_high)]

    plan = [
        (
            [where[(q % quarters, h)] for q in (e - 2, e - 1, e) for h in (0, 1)],
            [where[(e, h)] for h in (0, 1)],
        )
        for e in range(quarters)
    ]
    weights = (w_query, w_key, w_value)
    tables = (cosine, sine)
    made = [
        project(0, lots[0], tables, *weights),
        project(rows, lots[1] + lots[2], tables, *weights),
    ]
    made = [m[0] for m in made]
    last, pieces, opposite = project(
        3 * rows, lots[3], tables, *weights, (infos[2], first_wide, made, plan[2])
    )
    made.append(last)
    after, before = attend([infos[1], infos[3]], first_wide, made, [plan[1], plan[3]])
    received = [shifted(c, "ctx", e) for c, e in ((opposite, 2), (after, 1), (before, 3))]
    (partial,) = attend([infos[0]], first_wide, made, [plan[0]], w_out)

    anchors = jnp.arange(groups, dtype=jnp.int32)
    source = jnp.sum(jnp.where(destinations[None, :] == anchors[:, None], anchors[None, :], 0), axis=1)
    delivered, partial = routed(pieces, source, partial)
    attended = other_terms(received, (1, 0, 2), others, partial)
    delivered, attended = lax.optimization_barrier((delivered, attended))
    spots = tuple(where[(q, h)] for q in range(quarters) for h in (0, 1))
    shape = (quarters * rows, w_key.shape[1] + w_value.shape[1])
    kv_cache = assemble(spots, place, delivered, shape)
    return attended[None], kv_cache[None]


def solution(mesh):
    return jax.shard_map(
        shards,
        mesh=mesh,
        in_specs=(
            P("dp", "ctx", None),
            P("dp", "ctx"),
            P(),
            P(),
            P(None, "ctx"),
            P(None, "ctx"),
            P(None, "ctx"),
            P("ctx", None),
        ),
        out_specs=(P("dp", "ctx", None), P("dp", None, "ctx")),
        check_vma=False,
    )
```

```python
import functools
import math

import jax
import jax.numpy as jnp
from jax import lax
from jax.experimental import pallas as pl
from jax.experimental.pallas import tpu as pltpu
from jax.sharding import PartitionSpec as P

HD = 128
VMEM_LIMIT = 60 << 20
PROJECT_WEIGHT = 1
LAST_WEIGHT = 120


def shifted(value, axis, by):
    count = lax.axis_size(axis)
    return lax.ppermute(value, axis, [(i, (i + by) % count) for i in range(count)])


def normalised(rows, norm_gain):
    wide = rows.astype(jnp.float32)
    scale = lax.rsqrt(jnp.mean(wide * wide, axis=-1, keepdims=True) + 1e-05)
    return (wide * scale * norm_gain).astype(jnp.bfloat16)


def rotary_tables(positions):
    half = HD // 2
    inverse = 500000.0 ** (-2.0 * jnp.arange(half, dtype=jnp.float32) / HD)
    angles = positions[:, None] * inverse
    cosine, sine = jnp.cos(angles), jnp.sin(angles)
    return (
        jnp.concatenate([cosine, cosine], axis=-1),
        jnp.concatenate([-sine, sine], axis=-1),
    )


def project_kernel(part, plan, *refs):
    rows_ref, held, row_sems, sems = refs[-4:]
    parts = row_sems.shape[0]
    half_refs, refs = refs[:parts], refs[parts:]
    cos_ref, sin_ref, wq_ref, wk_ref, wv_ref = refs[:5]
    refs = refs[5:]
    if part == "all":
        (out_ref,) = refs[:1]
    elif part == "kv":
        own_ref, near_ref, out_ref, pieces_ref = refs[:4]
    else:
        info_ref, first_ref, own_ref, near_ref, far_ref, context_ref, out_ref = refs[:7]
    half = half_refs[0].shape[0]
    count, _, tile = held.shape
    has_kv = part != "q"
    shift = 2 if has_kv else 0

    def source(i):
        if has_kv and i < 2:
            return (wk_ref, wv_ref)[i]
        return wq_ref.at[:, pl.ds((i - shift) * tile, tile)]

    def start(i):
        pltpu.make_async_copy(source(i), held.at[i], sems.at[i]).start()

    moves = [
        pltpu.make_async_copy(ref, rows_ref.at[pl.ds(i * half, half)], row_sems.at[i])
        for i, ref in enumerate(half_refs)
    ]
    for move in moves:
        move.start()
    start(0)
    start(1)
    for move in moves:
        move.wait()

    def one(i, carry):
        pltpu.make_async_copy(wk_ref, held.at[i], sems.at[i]).wait()
        for k in range(2, count):
            pl.when(i == k - 2)(functools.partial(start, k))
        made = jnp.dot(rows_ref[...], held[i], preferred_element_type=jnp.float32)
        cosine, sine = cos_ref[...], sin_ref[...]
        slot = i
        if has_kv:
            cosine = jnp.where(i == 1, 1.0, cosine)
            sine = jnp.where(i == 1, 0.0, sine)
        if part == "all":
            slot = jnp.where(i < 2, i + count - 2, i - 2)
        for at in range(0, tile, HD):
            piece = made[:, at : at + HD]
            piece = piece * cosine + pltpu.roll(piece, HD // 2, 1) * sine
            out_ref[slot, :, at : at + HD] = piece.astype(out_ref.dtype)
        return carry

    lax.fori_loop(0, count, one, 0)
    if part == "all":
        return
    rows = own_ref.shape[1]
    kv_refs = [own_ref, near_ref.at[:, pl.ds(0, rows)], near_ref.at[:, pl.ds(rows, rows)]]
    if part == "kv":
        for kind in (0, 1):
            for slot, kv_ref in enumerate(kv_refs + [out_ref]):
                pieces_ref[kind * 16 : (kind + 1) * 16, slot * 16 : (slot + 1) * 16] = kv_ref[
                    kind
                ].reshape(16, 16, tile)
        return

    def store(head, block):
        context_ref[:, head * HD : (head + 1) * HD] = block

    attend_quarter(
        info_ref, first_ref, kv_refs + [far_ref], {plan[1][0][0]: out_ref}, *plan, store
    )


def whole(shape):
    return pl.BlockSpec(shape, lambda i: (0,) * len(shape))


def kv_block(array):
    last = array.shape[0] // 2 - 1
    return pl.BlockSpec((2,) + array.shape[1:], lambda i: (last, 0, 0))


def project(part, lot, arrived, tables, weights, kv=(), attend_with=None):
    w_query, w_key, w_value = weights
    rows, width = len(arrived) * arrived[0].shape[0], arrived[0].shape[1]
    tile = w_key.shape[1]
    q_tiles = w_query.shape[1] // tile
    count = {"all": q_tiles + 2, "kv": 2, "q": q_tiles}[part]
    anywhere = pl.BlockSpec(memory_space=pl.ANY)
    table = pl.BlockSpec((pl.Element(rows), pl.Element(HD)), lambda i: (lot, 0))
    operands = [*arrived, *tables, w_query, w_key, w_value]
    in_specs = [anywhere] * len(arrived) + [table] * 2 + [anywhere] * 3
    shapes = [(count, rows, tile)]
    scratch, plan = [], None
    if part == "kv":
        shapes.append((32, 64, tile))
    if part == "q":
        info, first_wide, plan = attend_with
        operands += [info, first_wide]
        in_specs += [pl.BlockSpec(memory_space=pltpu.SMEM), whole(first_wide.shape)]
        scratch = [pltpu.VMEM(shapes[0], jnp.bfloat16)]
        shapes = [(rows, q_tiles * tile)]
    operands += kv
    in_specs += [kv_block(array) for array in kv]
    weight = {"all": PROJECT_WEIGHT, "kv": LAST_WEIGHT, "q": 0}[part]
    return pl.pallas_call(
        functools.partial(project_kernel, part, plan),
        grid=(1,),
        in_specs=in_specs,
        out_specs=[whole(shape) for shape in shapes],
        out_shape=[jax.ShapeDtypeStruct(shape, jnp.bfloat16) for shape in shapes],
        scratch_shapes=scratch
        + [
            pltpu.VMEM((rows, width), jnp.bfloat16),
            pltpu.VMEM((count, width, tile), jnp.bfloat16),
            pltpu.SemaphoreType.DMA((len(arrived),)),
            pltpu.SemaphoreType.DMA((count,)),
        ],
        compiler_params=pltpu.CompilerParams(vmem_limit_bytes=VMEM_LIMIT),
        cost_estimate=pl.CostEstimate(
            flops=weight * 2 * rows * width * tile * count,
            bytes_accessed=2 * width * (tile * count + rows),
            transcendentals=0,
        ),
        name="project_" + part,
    )(*operands)


def attend_quarter(info_ref, first_ref, kv_refs, q_refs, slots, q_slots, store):
    blocks, base = info_ref[0], info_ref[1]
    half = first_ref.shape[0] // 8
    rows = 2 * half
    factor = math.log2(math.e) / math.sqrt(HD)
    first = jnp.concatenate(
        [first_ref[lot * rows + at : lot * rows + at + half, :1] for lot, at in q_slots], axis=0
    )

    def run(used):
        count = used * rows
        column = lax.broadcasted_iota(jnp.int32, (rows, count), 1) + (base + rows - count)
        line = lax.broadcasted_iota(jnp.int32, (rows, count), 0) + base
        bias = jnp.where((column >= first) & (column <= line), 0.0, -1e30)
        ones = jnp.ones((count, HD), jnp.bfloat16)
        pieces = slots[2 * (3 - used) :]
        for kv_head in range(2):
            place = slice(kv_head * HD, (kv_head + 1) * HD)
            keys = jnp.concatenate([kv_refs[a][0, at : at + half, place] for a, at in pieces], axis=0)
            values = jnp.concatenate(
                [kv_refs[a][1, at : at + half, place] for a, at in pieces], axis=0
            )
            values = jnp.concatenate([values, ones], axis=1)
            for head in range(4 * kv_head, 4 * kv_head + 4):
                within = slice(head % 2 * HD, (head % 2 + 1) * HD)
                queries = jnp.concatenate(
                    [q_refs[a][head // 2, at : at + half, within] for a, at in q_slots], axis=0
                )
                scores = lax.dot_general(
                    queries, keys, (((1,), (1,)), ((), ())), preferred_element_type=jnp.float32
                )
                scores = scores + bias
                most = jnp.max(scores, axis=-1, keepdims=True)
                weights = jnp.exp2((scores - most) * factor).astype(jnp.bfloat16)
                summed = jnp.dot(weights, values, preferred_element_type=jnp.float32)
                store(head, (summed[:, :HD] / summed[:, HD:]).astype(jnp.bfloat16))

    for used in (1, 2, 3):
        pl.when(blocks == used)(functools.partial(run, used))


def attend_kernel(plan, lots, *refs):
    quarters = len(plan)
    info_refs, first_ref = refs[:quarters], refs[quarters]
    own_ref, near_ref, far_ref = refs[quarters + 1 : quarters + 4]
    rows = own_ref.shape[1]
    kv_refs = [own_ref, near_ref.at[:, pl.ds(0, rows)], near_ref.at[:, pl.ds(rows, rows)], far_ref]
    refs = refs[quarters + 4 :]
    q_refs, out_refs = dict(zip(lots, refs)), refs[len(lots) :]
    for info_ref, out_ref, (slots, q_slots) in zip(info_refs, out_refs, plan):

        def store(head, block, out_ref=out_ref):
            out_ref[:, head * HD : (head + 1) * HD] = block

        attend_quarter(info_ref, first_ref, kv_refs, q_refs, slots, q_slots, store)


def attend_operands(infos, first_wide, kv, queries, plan):
    rows, tile = kv[0].shape[1:]
    tiles = queries[0][0].shape[0] - 2
    lots = [lot for _, _, lot in queries]
    spot = lambda n: pl.BlockSpec((tiles, rows, tile), lambda i: (0, n, 0))
    in_specs = (
        [pl.BlockSpec(memory_space=pltpu.SMEM)] * len(plan)
        + [whole(first_wide.shape)]
        + [kv_block(array) for array in kv]
        + [spot(n) for _, n, _ in queries]
    )
    return lots, in_specs, [*infos, first_wide, *kv, *[array for array, _, _ in queries]]


def attend(infos, first_wide, kv, queries, plan):
    rows, tile = kv[0].shape[1:]
    width = (queries[0][0].shape[0] - 2) * tile
    lots, in_specs, operands = attend_operands(infos, first_wide, kv, queries, plan)
    return pl.pallas_call(
        functools.partial(attend_kernel, plan, lots),
        grid=(1,),
        in_specs=in_specs,
        out_specs=[whole((rows, width))] * len(plan),
        out_shape=[jax.ShapeDtypeStruct((rows, width), jnp.bfloat16)] * len(plan),
        compiler_params=pltpu.CompilerParams(vmem_limit_bytes=VMEM_LIMIT),
        cost_estimate=pl.CostEstimate(flops=0, bytes_accessed=0, transcendentals=0),
        name="attend",
    )(*operands)


def out_kernel(order, *refs):
    stacked, held, sems, context_sems = refs[-4:]
    out_ref = refs[-5]
    w_out_ref, others_ref = refs[-7:-5]
    count = len(order)
    context_refs = refs[: count + 1]
    slots, _, tile = held.shape
    depth = w_out_ref.shape[0]
    steps = out_ref.shape[1] // tile

    def copies(step, slot):
        at = pl.ds(pl.multiple_of(step * tile, tile), tile)
        sources = [w_out_ref.at[:, at]] + [others_ref.at[index, :, at] for index in order]
        return [
            pltpu.make_async_copy(
                source, held.at[slot, pl.ds(i * depth, depth)], sems.at[slot, i]
            )
            for i, source in enumerate(sources)
        ]

    gathers = [
        pltpu.make_async_copy(
            ref, stacked.at[:, pl.ds(i * depth, depth)], context_sems.at[i]
        )
        for i, ref in enumerate(context_refs)
    ]
    for gather in gathers:
        gather.start()
    for step in range(slots - 1):
        for copy in copies(step, step):
            copy.start()
    for gather in gathers:
        gather.wait()

    def one(step, carry):
        slot = lax.rem(step, slots)
        for copy in copies(step, slot):
            copy.wait()

        @pl.when(step + slots - 1 < steps)
        def _():
            for copy in copies(step + slots - 1, lax.rem(step + slots - 1, slots)):
                copy.start()

        total = jnp.dot(stacked[...], held[slot], preferred_element_type=jnp.float32)
        out_ref[:, pl.ds(pl.multiple_of(step * tile, tile), tile)] = total.astype(out_ref.dtype)
        return carry

    lax.fori_loop(0, steps, one, 0)


def out_terms(contexts, order, w_out, others):
    rows, depth = contexts[0].shape
    width = w_out.shape[1]
    tile, slots, count = 512, 4, len(contexts)
    anywhere = pl.BlockSpec(memory_space=pl.ANY)
    return pl.pallas_call(
        functools.partial(out_kernel, order),
        grid=(1,),
        in_specs=[anywhere] * (count + 2),
        out_specs=whole((rows, width)),
        out_shape=jax.ShapeDtypeStruct((rows, width), jnp.bfloat16),
        scratch_shapes=[
            pltpu.VMEM((rows, count * depth), jnp.bfloat16),
            pltpu.VMEM((slots, count * depth, tile), jnp.bfloat16),
            pltpu.SemaphoreType.DMA((slots, count)),
            pltpu.SemaphoreType.DMA((count,)),
        ],
        compiler_params=pltpu.CompilerParams(vmem_limit_bytes=VMEM_LIMIT),
        cost_estimate=pl.CostEstimate(
            flops=2 * count * rows * depth * width,
            bytes_accessed=2 * count * depth * width,
            transcendentals=0,
        ),
        name="out_terms",
    )(*contexts, w_out, others)


def reorder_kernel(source_ref, in_ref, out_ref):
    def one(i, carry):
        out_ref[i] = in_ref[source_ref[i]]
        return carry

    lax.fori_loop(0, in_ref.shape[0], one, 0)


def routed(pieces, source):
    scattered = lax.all_to_all(pieces, "dp", 0, 0, tiled=False)
    ordered = pl.pallas_call(
        reorder_kernel,
        grid=(1,),
        in_specs=[pl.BlockSpec(memory_space=pltpu.SMEM), whole(pieces.shape)],
        out_specs=whole(pieces.shape),
        out_shape=jax.ShapeDtypeStruct(pieces.shape, pieces.dtype),
        name="reorder",
    )(source, scattered)
    return lax.all_to_all(ordered, "dp", 0, 0, tiled=False)


def assemble_kernel(spots, place_ref, pieces_ref, out_ref):
    quarters = len(spots) // 2
    rows = out_ref.shape[0] // quarters
    half = rows // 2
    for quarter in range(quarters):
        base = pl.multiple_of(lax.rem(place_ref[0] + quarter, quarters) * rows, rows)
        for which in (0, 1):
            slot, at = spots[2 * quarter + which]
            for kind in range(2):
                block = pieces_ref[
                    kind * 16 + at // 16 : kind * 16 + (at + half) // 16,
                    slot * 16 : (slot + 1) * 16,
                ].reshape(half, 2 * HD)
                for head in range(2):
                    to = (2 * head + kind) * HD
                    out_ref[pl.ds(base + which * half, half), to : to + HD] = block[
                        :, head * HD : (head + 1) * HD
                    ]


def assemble(spots, place, pieces, shape):
    return pl.pallas_call(
        functools.partial(assemble_kernel, spots),
        grid=(1,),
        in_specs=[pl.BlockSpec(memory_space=pltpu.SMEM), whole(pieces.shape)],
        out_specs=whole(shape),
        out_shape=jax.ShapeDtypeStruct(shape, pieces.dtype),
        name="assemble",
    )(jnp.reshape(place, (1,)).astype(jnp.int32), pieces)


def shards(tokens, doc_ids, destinations, norm_gain, w_query, w_key, w_value, w_out):
    quarters = lax.axis_size("ctx")
    groups = lax.axis_size("dp")
    place = lax.axis_index("ctx")
    row = lax.axis_index("dp")
    rows = tokens.shape[1]
    half = rows // 2

    ids = [doc_ids[0]] + [shifted(doc_ids[0], "ctx", -e) for e in range(1, quarters)]

    share = w_out.shape[0] // groups
    mine = lax.dynamic_slice_in_dim(w_out, row * share, share, 0)
    shares = jnp.stack([shifted(mine, "ctx", e) for e in range(1, quarters)])

    normed = normalised(tokens[0], norm_gain)
    low, high = normed[:half], normed[half:]
    shares, low, high, ids = lax.optimization_barrier((shares, low, high, ids))
    others = lax.all_gather(shares, "dp", axis=1, tiled=True)
    before_low, after_high = shifted(low, "ctx", 1), shifted(high, "ctx", -1)
    halves = [tuple((q, h) for h in (0, 1)) for q in (0, 1, 3, 2)]
    where = {h: (i, j * half) for i, pair in enumerate(halves) for j, h in enumerate(pair)}

    bases = [(place + e) % quarters * rows for e in range(quarters)]
    steps = jnp.arange(half, dtype=jnp.int32)
    order = [h for pair in halves for h in pair]
    row_index = jnp.concatenate([bases[q] + (h * half + steps) for q, h in order])
    row_ids = jnp.concatenate([ids[q][h * half : (h + 1) * half] for q, h in order])
    first = jnp.min(
        jnp.where(row_ids[:, None] == row_ids[None, :], row_index[None, :], quarters * rows), axis=-1
    )
    cosine, sine = rotary_tables((row_index - first).astype(jnp.float32))
    first_wide = jnp.broadcast_to(first[:, None], (first.shape[0], HD))
    infos = []
    for e in range(quarters):
        lot, at = where[(e, 0)]
        least = first[lot * rows + at]
        count = 1 + (least < bases[e]).astype(jnp.int32) + (least < bases[e] - rows).astype(jnp.int32)
        infos.append(jnp.stack([count, bases[e]]))
    anchors = jnp.arange(groups, dtype=jnp.int32)
    source = jnp.sum(jnp.where(destinations[None, :] == anchors[:, None], anchors[None, :], 0), axis=1)
    cosine, sine, first_wide, infos, source = lax.optimization_barrier(
        (cosine, sine, first_wide, infos, source)
    )

    plan = [
        (
            [where[(q % quarters, h)] for q in (e - 2, e - 1, e) for h in (0, 1)],
            [where[(e, h)] for h in (0, 1)],
        )
        for e in range(quarters)
    ]
    weights = (w_query, w_key, w_value)
    tables = (cosine, sine)
    then_low, then_high, _ = lax.optimization_barrier((low, high, first))
    before_high, after_low = shifted(then_high, "ctx", 1), shifted(then_low, "ctx", -1)
    (own,) = project("all", 0, (low, high), tables, weights)
    before_low, after_high, own = lax.optimization_barrier((before_low, after_high, own))
    far = (shifted(before_low, "ctx", 1), shifted(after_high, "ctx", -1))
    arrived = (after_low, after_high, before_low, before_high)
    (near,) = project("all", rows, arrived, tables, weights)
    far_kv, pieces = project("kv", 3 * rows, far, tables, weights, (own, near))
    kv = (own, near, far_kv)
    (opposite,) = project(
        "q", 3 * rows, far, tables, weights, kv, (infos[2], first_wide, plan[2])
    )
    queries = [(near, 0, 1), (near, 1, 2)]
    next_one, previous = attend(
        [infos[1], infos[3]], first_wide, kv, queries, [plan[1], plan[3]]
    )
    received = [shifted(c, "ctx", e) for c, e in ((opposite, 2), (next_one, 1), (previous, 3))]

    delivered = routed(pieces, source)
    (mine_context,) = attend([infos[0]], first_wide, kv, [(own, 0, 0)], [plan[0]])
    attended = out_terms([mine_context, *received], (1, 0, 2), w_out, others)
    delivered, attended = lax.optimization_barrier((delivered, attended))
    spots = tuple(where[(q, h)] for q in range(quarters) for h in (0, 1))
    shape = (quarters * rows, w_key.shape[1] + w_value.shape[1])
    kv_cache = assemble(spots, place, delivered, shape)
    return attended[None], kv_cache[None]


def solution(mesh):
    return jax.shard_map(
        shards,
        mesh=mesh,
        in_specs=(
            P("dp", "ctx", None),
            P("dp", "ctx"),
            P(),
            P(),
            P(None, "ctx"),
            P(None, "ctx"),
            P(None, "ctx"),
            P("ctx", None),
        ),
        out_specs=(P("dp", "ctx", None), P("dp", None, "ctx")),
        check_vma=False,
    )
```

```python
import functools
import math

import jax
import jax.numpy as jnp
from jax import lax
from jax.experimental import pallas as pl
from jax.experimental.pallas import tpu as pltpu
from jax.sharding import PartitionSpec as P

HD = 128
VMEM_LIMIT = 60 << 20
PROJECT_WEIGHT = 1
LAST_WEIGHT = 120


def shifted(value, axis, by):
    count = lax.axis_size(axis)
    return lax.ppermute(value, axis, [(i, (i + by) % count) for i in range(count)])


def normalised(rows, norm_gain):
    wide = rows.astype(jnp.float32)
    scale = lax.rsqrt(jnp.mean(wide * wide, axis=-1, keepdims=True) + 1e-05)
    return (wide * scale * norm_gain).astype(jnp.bfloat16)


def rotary_tables(positions):
    half = HD // 2
    inverse = 500000.0 ** (-2.0 * jnp.arange(half, dtype=jnp.float32) / HD)
    angles = positions[:, None] * inverse
    cosine, sine = jnp.cos(angles), jnp.sin(angles)
    return (
        jnp.concatenate([cosine, cosine], axis=-1),
        jnp.concatenate([-sine, sine], axis=-1),
    )


def project_kernel(part, plan, *refs):
    rows_ref, held, row_sems, sems = refs[-4:]
    parts = row_sems.shape[0]
    half_refs, refs = refs[:parts], refs[parts:]
    cos_ref, sin_ref, wq_ref, wk_ref, wv_ref = refs[:5]
    refs = refs[5:]
    if part == "all":
        (out_ref,) = refs[:1]
    elif part == "kv":
        own_ref, near_ref, out_ref, pieces_ref = refs[:4]
    else:
        info_ref, first_ref, own_ref, near_ref, far_ref, context_ref, out_ref = refs[:7]
    half = half_refs[0].shape[0]
    count, _, tile = held.shape
    has_kv = part != "q"
    shift = 2 if has_kv else 0

    def source(i):
        if has_kv and i < 2:
            return (wk_ref, wv_ref)[i]
        return wq_ref.at[:, pl.ds((i - shift) * tile, tile)]

    def start(i):
        pltpu.make_async_copy(source(i), held.at[i], sems.at[i]).start()

    moves = [
        pltpu.make_async_copy(ref, rows_ref.at[pl.ds(i * half, half)], row_sems.at[i])
        for i, ref in enumerate(half_refs)
    ]
    for move in moves:
        move.start()
    start(0)
    start(1)
    for move in moves:
        move.wait()

    def one(i, carry):
        pltpu.make_async_copy(wk_ref, held.at[i], sems.at[i]).wait()
        for k in range(2, count):
            pl.when(i == k - 2)(functools.partial(start, k))
        made = jnp.dot(rows_ref[...], held[i], preferred_element_type=jnp.float32)
        cosine, sine = cos_ref[...], sin_ref[...]
        slot = i
        if has_kv:
            cosine = jnp.where(i == 1, 1.0, cosine)
            sine = jnp.where(i == 1, 0.0, sine)
        if part == "all":
            slot = jnp.where(i < 2, i + count - 2, i - 2)
        for at in range(0, tile, HD):
            piece = made[:, at : at + HD]
            piece = piece * cosine + pltpu.roll(piece, HD // 2, 1) * sine
            out_ref[slot, :, at : at + HD] = piece.astype(out_ref.dtype)
        return carry

    lax.fori_loop(0, count, one, 0)
    if part == "all":
        return
    rows = own_ref.shape[1]
    kv_refs = [own_ref, near_ref.at[:, pl.ds(0, rows)], near_ref.at[:, pl.ds(rows, rows)]]
    if part == "kv":
        for kind in (0, 1):
            for slot, kv_ref in enumerate(kv_refs + [out_ref]):
                pieces_ref[kind * 16 : (kind + 1) * 16, slot * 16 : (slot + 1) * 16] = kv_ref[
                    kind
                ].reshape(16, 16, tile)
        return

    def store(head, block):
        context_ref[:, head * HD : (head + 1) * HD] = block

    attend_quarter(
        info_ref, first_ref, kv_refs + [far_ref], {plan[1][0][0]: out_ref}, *plan, store
    )


def whole(shape):
    return pl.BlockSpec(shape, lambda i: (0,) * len(shape))


def kv_block(array):
    last = array.shape[0] // 2 - 1
    return pl.BlockSpec((2,) + array.shape[1:], lambda i: (last, 0, 0))


def project(part, lot, arrived, tables, weights, kv=(), attend_with=None):
    w_query, w_key, w_value = weights
    rows, width = len(arrived) * arrived[0].shape[0], arrived[0].shape[1]
    tile = w_key.shape[1]
    q_tiles = w_query.shape[1] // tile
    count = {"all": q_tiles + 2, "kv": 2, "q": q_tiles}[part]
    anywhere = pl.BlockSpec(memory_space=pl.ANY)
    table = pl.BlockSpec((pl.Element(rows), pl.Element(HD)), lambda i: (lot, 0))
    operands = [*arrived, *tables, w_query, w_key, w_value]
    in_specs = [anywhere] * len(arrived) + [table] * 2 + [anywhere] * 3
    shapes = [(count, rows, tile)]
    scratch, plan = [], None
    if part == "kv":
        shapes.append((32, 64, tile))
    if part == "q":
        info, first_wide, plan = attend_with
        operands += [info, first_wide]
        in_specs += [pl.BlockSpec(memory_space=pltpu.SMEM), whole(first_wide.shape)]
        scratch = [pltpu.VMEM(shapes[0], jnp.bfloat16)]
        shapes = [(rows, q_tiles * tile)]
    operands += kv
    in_specs += [kv_block(array) for array in kv]
    weight = {"all": PROJECT_WEIGHT, "kv": LAST_WEIGHT, "q": 0}[part]
    return pl.pallas_call(
        functools.partial(project_kernel, part, plan),
        grid=(1,),
        in_specs=in_specs,
        out_specs=[whole(shape) for shape in shapes],
        out_shape=[jax.ShapeDtypeStruct(shape, jnp.bfloat16) for shape in shapes],
        scratch_shapes=scratch
        + [
            pltpu.VMEM((rows, width), jnp.bfloat16),
            pltpu.VMEM((count, width, tile), jnp.bfloat16),
            pltpu.SemaphoreType.DMA((len(arrived),)),
            pltpu.SemaphoreType.DMA((count,)),
        ],
        compiler_params=pltpu.CompilerParams(vmem_limit_bytes=VMEM_LIMIT),
        cost_estimate=pl.CostEstimate(
            flops=weight * 2 * rows * width * tile * count,
            bytes_accessed=2 * width * (tile * count + rows),
            transcendentals=0,
        ),
        name="project_" + part,
    )(*operands)


def attend_quarter(info_ref, first_ref, kv_refs, q_refs, slots, q_slots, store):
    blocks, base = info_ref[0], info_ref[1]
    half = first_ref.shape[0] // 8
    rows = 2 * half
    factor = math.log2(math.e) / math.sqrt(HD)
    first = jnp.concatenate(
        [first_ref[lot * rows + at : lot * rows + at + half, :1] for lot, at in q_slots], axis=0
    )

    def run(used):
        count = used * rows
        column = lax.broadcasted_iota(jnp.int32, (rows, count), 1) + (base + rows - count)
        line = lax.broadcasted_iota(jnp.int32, (rows, count), 0) + base
        bias = jnp.where((column >= first) & (column <= line), 0.0, -1e30)
        ones = jnp.ones((count, HD), jnp.bfloat16)
        pieces = slots[2 * (3 - used) :]
        for kv_head in range(2):
            place = slice(kv_head * HD, (kv_head + 1) * HD)
            keys = jnp.concatenate([kv_refs[a][0, at : at + half, place] for a, at in pieces], axis=0)
            values = jnp.concatenate(
                [kv_refs[a][1, at : at + half, place] for a, at in pieces], axis=0
            )
            values = jnp.concatenate([values, ones], axis=1)
            for head in range(4 * kv_head, 4 * kv_head + 4):
                within = slice(head % 2 * HD, (head % 2 + 1) * HD)
                queries = jnp.concatenate(
                    [q_refs[a][head // 2, at : at + half, within] for a, at in q_slots], axis=0
                )
                scores = lax.dot_general(
                    queries, keys, (((1,), (1,)), ((), ())), preferred_element_type=jnp.float32
                )
                scores = scores + bias
                most = jnp.max(scores, axis=-1, keepdims=True)
                weights = jnp.exp2((scores - most) * factor).astype(jnp.bfloat16)
                summed = jnp.dot(weights, values, preferred_element_type=jnp.float32)
                store(head, (summed[:, :HD] / summed[:, HD:]).astype(jnp.bfloat16))

    for used in (1, 2, 3):
        pl.when(blocks == used)(functools.partial(run, used))


def attend_kernel(plan, lots, *refs):
    quarters = len(plan)
    info_refs, first_ref = refs[:quarters], refs[quarters]
    own_ref, near_ref, far_ref = refs[quarters + 1 : quarters + 4]
    rows = own_ref.shape[1]
    kv_refs = [own_ref, near_ref.at[:, pl.ds(0, rows)], near_ref.at[:, pl.ds(rows, rows)], far_ref]
    refs = refs[quarters + 4 :]
    q_refs, out_refs = dict(zip(lots, refs)), refs[len(lots) :]
    for info_ref, out_ref, (slots, q_slots) in zip(info_refs, out_refs, plan):

        def store(head, block, out_ref=out_ref):
            out_ref[:, head * HD : (head + 1) * HD] = block

        attend_quarter(info_ref, first_ref, kv_refs, q_refs, slots, q_slots, store)


def attend_operands(infos, first_wide, kv, queries, plan):
    rows, tile = kv[0].shape[1:]
    tiles = queries[0][0].shape[0] - 2
    lots = [lot for _, _, lot in queries]
    spot = lambda n: pl.BlockSpec((tiles, rows, tile), lambda i: (0, n, 0))
    in_specs = (
        [pl.BlockSpec(memory_space=pltpu.SMEM)] * len(plan)
        + [whole(first_wide.shape)]
        + [kv_block(array) for array in kv]
        + [spot(n) for _, n, _ in queries]
    )
    return lots, in_specs, [*infos, first_wide, *kv, *[array for array, _, _ in queries]]


def attend(infos, first_wide, kv, queries, plan):
    rows, tile = kv[0].shape[1:]
    width = (queries[0][0].shape[0] - 2) * tile
    lots, in_specs, operands = attend_operands(infos, first_wide, kv, queries, plan)
    return pl.pallas_call(
        functools.partial(attend_kernel, plan, lots),
        grid=(1,),
        in_specs=in_specs,
        out_specs=[whole((rows, width))] * len(plan),
        out_shape=[jax.ShapeDtypeStruct((rows, width), jnp.bfloat16)] * len(plan),
        compiler_params=pltpu.CompilerParams(vmem_limit_bytes=VMEM_LIMIT),
        cost_estimate=pl.CostEstimate(flops=0, bytes_accessed=0, transcendentals=0),
        name="attend",
    )(*operands)


def out_kernel(order, *refs):
    stacked, held, sems, context_sems = refs[-4:]
    out_ref = refs[-5]
    w_out_ref, others_ref = refs[-7:-5]
    count = len(order)
    context_refs = refs[: count + 1]
    slots, _, tile = held.shape
    depth = w_out_ref.shape[0]
    steps = out_ref.shape[1] // tile

    def copies(step, slot):
        at = pl.ds(pl.multiple_of(step * tile, tile), tile)
        sources = [w_out_ref.at[:, at]] + [others_ref.at[index, :, at] for index in order]
        return [
            pltpu.make_async_copy(
                source, held.at[slot, pl.ds(i * depth, depth)], sems.at[slot, i]
            )
            for i, source in enumerate(sources)
        ]

    gathers = [
        pltpu.make_async_copy(
            ref, stacked.at[:, pl.ds(i * depth, depth)], context_sems.at[i]
        )
        for i, ref in enumerate(context_refs)
    ]
    for gather in gathers:
        gather.start()
    for step in range(slots - 1):
        for copy in copies(step, step):
            copy.start()
    for gather in gathers:
        gather.wait()

    def one(step, carry):
        slot = lax.rem(step, slots)
        for copy in copies(step, slot):
            copy.wait()

        @pl.when(step + slots - 1 < steps)
        def _():
            for copy in copies(step + slots - 1, lax.rem(step + slots - 1, slots)):
                copy.start()

        total = jnp.dot(stacked[...], held[slot], preferred_element_type=jnp.float32)
        out_ref[:, pl.ds(pl.multiple_of(step * tile, tile), tile)] = total.astype(out_ref.dtype)
        return carry

    lax.fori_loop(0, steps, one, 0)


def out_terms(contexts, order, w_out, others):
    rows, depth = contexts[0].shape
    width = w_out.shape[1]
    tile, slots, count = 512, 3, len(contexts)
    anywhere = pl.BlockSpec(memory_space=pl.ANY)
    return pl.pallas_call(
        functools.partial(out_kernel, order),
        grid=(1,),
        in_specs=[anywhere] * (count + 2),
        out_specs=whole((rows, width)),
        out_shape=jax.ShapeDtypeStruct((rows, width), jnp.bfloat16),
        scratch_shapes=[
            pltpu.VMEM((rows, count * depth), jnp.bfloat16),
            pltpu.VMEM((slots, count * depth, tile), jnp.bfloat16),
            pltpu.SemaphoreType.DMA((slots, count)),
            pltpu.SemaphoreType.DMA((count,)),
        ],
        compiler_params=pltpu.CompilerParams(vmem_limit_bytes=VMEM_LIMIT),
        cost_estimate=pl.CostEstimate(
            flops=2 * count * rows * depth * width,
            bytes_accessed=2 * count * depth * width,
            transcendentals=0,
        ),
        name="out_terms",
    )(*contexts, w_out, others)


def reorder_kernel(source_ref, in_ref, out_ref):
    def one(i, carry):
        out_ref[i] = in_ref[source_ref[i]]
        return carry

    lax.fori_loop(0, in_ref.shape[0], one, 0)


def routed(pieces, source):
    scattered = lax.all_to_all(pieces, "dp", 0, 0, tiled=False)
    ordered = pl.pallas_call(
        reorder_kernel,
        grid=(1,),
        in_specs=[pl.BlockSpec(memory_space=pltpu.SMEM), whole(pieces.shape)],
        out_specs=whole(pieces.shape),
        out_shape=jax.ShapeDtypeStruct(pieces.shape, pieces.dtype),
        name="reorder",
    )(source, scattered)
    return lax.all_to_all(ordered, "dp", 0, 0, tiled=False)


def assemble_kernel(spots, place_ref, pieces_ref, out_ref):
    quarters = len(spots) // 2
    rows = out_ref.shape[0] // quarters
    half = rows // 2
    for quarter in range(quarters):
        base = pl.multiple_of(lax.rem(place_ref[0] + quarter, quarters) * rows, rows)
        for which in (0, 1):
            slot, at = spots[2 * quarter + which]
            for kind in range(2):
                block = pieces_ref[
                    kind * 16 + at // 16 : kind * 16 + (at + half) // 16,
                    slot * 16 : (slot + 1) * 16,
                ].reshape(half, 2 * HD)
                for head in range(2):
                    to = (2 * head + kind) * HD
                    out_ref[pl.ds(base + which * half, half), to : to + HD] = block[
                        :, head * HD : (head + 1) * HD
                    ]


def assemble(spots, place, pieces, shape):
    return pl.pallas_call(
        functools.partial(assemble_kernel, spots),
        grid=(1,),
        in_specs=[pl.BlockSpec(memory_space=pltpu.SMEM), whole(pieces.shape)],
        out_specs=whole(shape),
        out_shape=jax.ShapeDtypeStruct(shape, pieces.dtype),
        compiler_params=pltpu.CompilerParams(vmem_limit_bytes=16 << 20),
        name="assemble",
    )(jnp.reshape(place, (1,)).astype(jnp.int32), pieces)


def shards(tokens, doc_ids, destinations, norm_gain, w_query, w_key, w_value, w_out):
    quarters = lax.axis_size("ctx")
    groups = lax.axis_size("dp")
    place = lax.axis_index("ctx")
    row = lax.axis_index("dp")
    rows = tokens.shape[1]
    half = rows // 2

    ids = [doc_ids[0]] + [shifted(doc_ids[0], "ctx", -e) for e in range(1, quarters)]

    share = w_out.shape[0] // groups
    mine = lax.dynamic_slice_in_dim(w_out, row * share, share, 0)
    shares = jnp.stack([shifted(mine, "ctx", e) for e in range(1, quarters)])

    normed = normalised(tokens[0], norm_gain)
    low, high = normed[:half], normed[half:]
    shares, low, high, ids = lax.optimization_barrier((shares, low, high, ids))
    others = lax.all_gather(shares, "dp", axis=1, tiled=True)
    before_low, after_high = shifted(low, "ctx", 1), shifted(high, "ctx", -1)
    halves = [tuple((q, h) for h in (0, 1)) for q in (0, 1, 3, 2)]
    where = {h: (i, j * half) for i, pair in enumerate(halves) for j, h in enumerate(pair)}

    bases = [(place + e) % quarters * rows for e in range(quarters)]
    steps = jnp.arange(half, dtype=jnp.int32)
    order = [h for pair in halves for h in pair]
    row_index = jnp.concatenate([bases[q] + (h * half + steps) for q, h in order])
    row_ids = jnp.concatenate([ids[q][h * half : (h + 1) * half] for q, h in order])
    first = jnp.min(
        jnp.where(row_ids[:, None] == row_ids[None, :], row_index[None, :], quarters * rows), axis=-1
    )
    cosine, sine = rotary_tables((row_index - first).astype(jnp.float32))
    first_wide = jnp.broadcast_to(first[:, None], (first.shape[0], HD))
    infos = []
    for e in range(quarters):
        lot, at = where[(e, 0)]
        least = first[lot * rows + at]
        count = 1 + (least < bases[e]).astype(jnp.int32) + (least < bases[e] - rows).astype(jnp.int32)
        infos.append(jnp.stack([count, bases[e]]))
    anchors = jnp.arange(groups, dtype=jnp.int32)
    source = jnp.sum(jnp.where(destinations[None, :] == anchors[:, None], anchors[None, :], 0), axis=1)
    cosine, sine, first_wide, infos, source = lax.optimization_barrier(
        (cosine, sine, first_wide, infos, source)
    )

    plan = [
        (
            [where[(q % quarters, h)] for q in (e - 2, e - 1, e) for h in (0, 1)],
            [where[(e, h)] for h in (0, 1)],
        )
        for e in range(quarters)
    ]
    weights = (w_query, w_key, w_value)
    tables = (cosine, sine)
    then_low, then_high, _ = lax.optimization_barrier((low, high, first))
    before_high, after_low = shifted(then_high, "ctx", 1), shifted(then_low, "ctx", -1)
    (own,) = project("all", 0, (low, high), tables, weights)
    before_low, after_high, own = lax.optimization_barrier((before_low, after_high, own))
    far = (shifted(before_low, "ctx", 1), shifted(after_high, "ctx", -1))
    arrived = (after_low, after_high, before_low, before_high)
    (near,) = project("all", rows, arrived, tables, weights)
    (next_one,) = attend([infos[1]], first_wide, (own, near, own), [(near, 0, 1)], [plan[1]])
    *far, next_one = lax.optimization_barrier((*far, next_one))
    far_kv, pieces = project("kv", 3 * rows, far, tables, weights, (own, near))
    kv = (own, near, far_kv)
    (opposite,) = project(
        "q", 3 * rows, far, tables, weights, kv, (infos[2], first_wide, plan[2])
    )
    (previous,) = attend([infos[3]], first_wide, kv, [(near, 1, 2)], [plan[3]])
    received = [shifted(c, "ctx", e) for c, e in ((opposite, 2), (next_one, 1), (previous, 3))]

    delivered = routed(pieces, source)
    (mine_context,) = attend([infos[0]], first_wide, kv, [(own, 0, 0)], [plan[0]])
    attended = out_terms([mine_context, *received], (1, 0, 2), w_out, others)
    delivered, attended = lax.optimization_barrier((delivered, attended))
    spots = tuple(where[(q, h)] for q in range(quarters) for h in (0, 1))
    shape = (quarters * rows, w_key.shape[1] + w_value.shape[1])
    kv_cache = assemble(spots, place, delivered, shape)
    return attended[None], kv_cache[None]


def solution(mesh):
    return jax.shard_map(
        shards,
        mesh=mesh,
        in_specs=(
            P("dp", "ctx", None),
            P("dp", "ctx"),
            P(),
            P(),
            P(None, "ctx"),
            P(None, "ctx"),
            P(None, "ctx"),
            P("ctx", None),
        ),
        out_specs=(P("dp", "ctx", None), P("dp", None, "ctx")),
        check_vma=False,
    )
```

```python
import functools
import math

import jax
import jax.numpy as jnp
from jax import lax
from jax.experimental import pallas as pl
from jax.experimental.pallas import tpu as pltpu
from jax.sharding import PartitionSpec as P

HD = 128
VMEM_LIMIT = 60 << 20
PROJECT_WEIGHT = 50
LAST_WEIGHT = 120


def shifted(value, axis, by):
    count = lax.axis_size(axis)
    return lax.ppermute(value, axis, [(i, (i + by) % count) for i in range(count)])


def normalised(rows, norm_gain):
    wide = rows.astype(jnp.float32)
    scale = lax.rsqrt(jnp.mean(wide * wide, axis=-1, keepdims=True) + 1e-05)
    return (wide * scale * norm_gain).astype(jnp.bfloat16)


def rotary_tables(positions):
    half = HD // 2
    inverse = 500000.0 ** (-2.0 * jnp.arange(half, dtype=jnp.float32) / HD)
    angles = positions[:, None] * inverse
    cosine, sine = jnp.cos(angles), jnp.sin(angles)
    return (
        jnp.concatenate([cosine, cosine], axis=-1),
        jnp.concatenate([-sine, sine], axis=-1),
    )


def project_kernel(part, plan, *refs):
    rows_ref, held, row_sems, sems = refs[-4:]
    parts = row_sems.shape[0]
    half_refs, refs = refs[:parts], refs[parts:]
    cos_ref, sin_ref, wq_ref, wk_ref, wv_ref = refs[:5]
    refs = refs[5:]
    if part == "all":
        (out_ref,) = refs[:1]
    elif part == "kv":
        own_ref, near_ref, out_ref, pieces_ref = refs[:4]
    else:
        info_ref, first_ref, own_ref, near_ref, far_ref, context_ref, out_ref = refs[:7]
    half = half_refs[0].shape[0]
    count, _, tile = held.shape
    has_kv = part != "q"
    shift = 2 if has_kv else 0

    def source(i):
        if has_kv and i < 2:
            return (wk_ref, wv_ref)[i]
        return wq_ref.at[:, pl.ds((i - shift) * tile, tile)]

    def start(i):
        pltpu.make_async_copy(source(i), held.at[i], sems.at[i]).start()

    moves = [
        pltpu.make_async_copy(ref, rows_ref.at[pl.ds(i * half, half)], row_sems.at[i])
        for i, ref in enumerate(half_refs)
    ]
    for move in moves:
        move.start()
    start(0)
    start(1)
    for move in moves:
        move.wait()

    def one(i, carry):
        pltpu.make_async_copy(wk_ref, held.at[i], sems.at[i]).wait()
        for k in range(2, count):
            pl.when(i == k - 2)(functools.partial(start, k))
        made = jnp.dot(rows_ref[...], held[i], preferred_element_type=jnp.float32)
        cosine, sine = cos_ref[...], sin_ref[...]
        slot = i
        if has_kv:
            cosine = jnp.where(i == 1, 1.0, cosine)
            sine = jnp.where(i == 1, 0.0, sine)
        if part == "all":
            slot = jnp.where(i < 2, i + count - 2, i - 2)
        for at in range(0, tile, HD):
            piece = made[:, at : at + HD]
            piece = piece * cosine + pltpu.roll(piece, HD // 2, 1) * sine
            out_ref[slot, :, at : at + HD] = piece.astype(out_ref.dtype)
        return carry

    lax.fori_loop(0, count, one, 0)
    if part == "all":
        return
    rows = own_ref.shape[1]
    kv_refs = [own_ref, near_ref.at[:, pl.ds(0, rows)], near_ref.at[:, pl.ds(rows, rows)]]
    if part == "kv":
        for kind in (0, 1):
            for slot, kv_ref in enumerate(kv_refs + [out_ref]):
                pieces_ref[kind * 16 : (kind + 1) * 16, slot * 16 : (slot + 1) * 16] = kv_ref[
                    kind
                ].reshape(16, 16, tile)
        return

    def store(head, block):
        context_ref[:, head * HD : (head + 1) * HD] = block

    attend_quarter(
        info_ref, first_ref, kv_refs + [far_ref], {plan[1][0][0]: out_ref}, *plan, store
    )


def whole(shape):
    return pl.BlockSpec(shape, lambda i: (0,) * len(shape))


def kv_block(array):
    last = array.shape[0] // 2 - 1
    return pl.BlockSpec((2,) + array.shape[1:], lambda i: (last, 0, 0))


def project(part, lot, arrived, tables, weights, kv=(), attend_with=None):
    w_query, w_key, w_value = weights
    rows, width = len(arrived) * arrived[0].shape[0], arrived[0].shape[1]
    tile = w_key.shape[1]
    q_tiles = w_query.shape[1] // tile
    count = {"all": q_tiles + 2, "kv": 2, "q": q_tiles}[part]
    anywhere = pl.BlockSpec(memory_space=pl.ANY)
    table = pl.BlockSpec((pl.Element(rows), pl.Element(HD)), lambda i: (lot, 0))
    operands = [*arrived, *tables, w_query, w_key, w_value]
    in_specs = [anywhere] * len(arrived) + [table] * 2 + [anywhere] * 3
    shapes = [(count, rows, tile)]
    scratch, plan = [], None
    if part == "kv":
        shapes.append((32, 64, tile))
    if part == "q":
        info, first_wide, plan = attend_with
        operands += [info, first_wide]
        in_specs += [pl.BlockSpec(memory_space=pltpu.SMEM), whole(first_wide.shape)]
        scratch = [pltpu.VMEM(shapes[0], jnp.bfloat16)]
        shapes = [(rows, q_tiles * tile)]
    operands += kv
    in_specs += [kv_block(array) for array in kv]
    weight = {"all": PROJECT_WEIGHT, "kv": LAST_WEIGHT, "q": 0}[part]
    return pl.pallas_call(
        functools.partial(project_kernel, part, plan),
        grid=(1,),
        in_specs=in_specs,
        out_specs=[whole(shape) for shape in shapes],
        out_shape=[jax.ShapeDtypeStruct(shape, jnp.bfloat16) for shape in shapes],
        scratch_shapes=scratch
        + [
            pltpu.VMEM((rows, width), jnp.bfloat16),
            pltpu.VMEM((count, width, tile), jnp.bfloat16),
            pltpu.SemaphoreType.DMA((len(arrived),)),
            pltpu.SemaphoreType.DMA((count,)),
        ],
        compiler_params=pltpu.CompilerParams(vmem_limit_bytes=VMEM_LIMIT),
        cost_estimate=pl.CostEstimate(
            flops=weight * 2 * rows * width * tile * count,
            bytes_accessed=2 * width * (tile * count + rows),
            transcendentals=0,
        ),
        name="project_" + part,
    )(*operands)


def attend_quarter(info_ref, first_ref, kv_refs, q_refs, slots, q_slots, store):
    blocks, base = info_ref[0], info_ref[1]
    half = first_ref.shape[0] // 8
    rows = 2 * half
    factor = math.log2(math.e) / math.sqrt(HD)
    first = jnp.concatenate(
        [first_ref[lot * rows + at : lot * rows + at + half, :1] for lot, at in q_slots], axis=0
    )

    def run(used):
        count = used * rows
        column = lax.broadcasted_iota(jnp.int32, (rows, count), 1) + (base + rows - count)
        line = lax.broadcasted_iota(jnp.int32, (rows, count), 0) + base
        bias = jnp.where((column >= first) & (column <= line), 0.0, -1e30)
        ones = jnp.ones((count, HD), jnp.bfloat16)
        pieces = slots[2 * (3 - used) :]
        for kv_head in range(2):
            place = slice(kv_head * HD, (kv_head + 1) * HD)
            keys = jnp.concatenate([kv_refs[a][0, at : at + half, place] for a, at in pieces], axis=0)
            values = jnp.concatenate(
                [kv_refs[a][1, at : at + half, place] for a, at in pieces], axis=0
            )
            values = jnp.concatenate([values, ones], axis=1)
            for head in range(4 * kv_head, 4 * kv_head + 4):
                within = slice(head % 2 * HD, (head % 2 + 1) * HD)
                queries = jnp.concatenate(
                    [q_refs[a][head // 2, at : at + half, within] for a, at in q_slots], axis=0
                )
                scores = lax.dot_general(
                    queries, keys, (((1,), (1,)), ((), ())), preferred_element_type=jnp.float32
                )
                scores = scores + bias
                most = jnp.max(scores, axis=-1, keepdims=True)
                weights = jnp.exp2((scores - most) * factor).astype(jnp.bfloat16)
                summed = jnp.dot(weights, values, preferred_element_type=jnp.float32)
                store(head, (summed[:, :HD] / summed[:, HD:]).astype(jnp.bfloat16))

    for used in (1, 2, 3):
        pl.when(blocks == used)(functools.partial(run, used))


def attend_kernel(plan, lots, *refs):
    quarters = len(plan)
    info_refs, first_ref = refs[:quarters], refs[quarters]
    own_ref, near_ref, far_ref = refs[quarters + 1 : quarters + 4]
    rows = own_ref.shape[1]
    kv_refs = [own_ref, near_ref.at[:, pl.ds(0, rows)], near_ref.at[:, pl.ds(rows, rows)], far_ref]
    refs = refs[quarters + 4 :]
    q_refs, out_refs = dict(zip(lots, refs)), refs[len(lots) :]
    for info_ref, out_ref, (slots, q_slots) in zip(info_refs, out_refs, plan):

        def store(head, block, out_ref=out_ref):
            out_ref[:, head * HD : (head + 1) * HD] = block

        attend_quarter(info_ref, first_ref, kv_refs, q_refs, slots, q_slots, store)


def attend_operands(infos, first_wide, kv, queries, plan):
    rows, tile = kv[0].shape[1:]
    tiles = queries[0][0].shape[0] - 2
    lots = [lot for _, _, lot in queries]
    spot = lambda n: pl.BlockSpec((tiles, rows, tile), lambda i: (0, n, 0))
    in_specs = (
        [pl.BlockSpec(memory_space=pltpu.SMEM)] * len(plan)
        + [whole(first_wide.shape)]
        + [kv_block(array) for array in kv]
        + [spot(n) for _, n, _ in queries]
    )
    return lots, in_specs, [*infos, first_wide, *kv, *[array for array, _, _ in queries]]


def attend(infos, first_wide, kv, queries, plan):
    rows, tile = kv[0].shape[1:]
    width = (queries[0][0].shape[0] - 2) * tile
    lots, in_specs, operands = attend_operands(infos, first_wide, kv, queries, plan)
    return pl.pallas_call(
        functools.partial(attend_kernel, plan, lots),
        grid=(1,),
        in_specs=in_specs,
        out_specs=[whole((rows, width))] * len(plan),
        out_shape=[jax.ShapeDtypeStruct((rows, width), jnp.bfloat16)] * len(plan),
        compiler_params=pltpu.CompilerParams(vmem_limit_bytes=VMEM_LIMIT),
        cost_estimate=pl.CostEstimate(flops=0, bytes_accessed=0, transcendentals=0),
        name="attend",
    )(*operands)


def out_kernel(order, *refs):
    stacked, held, sems, context_sems = refs[-4:]
    out_ref = refs[-5]
    w_out_ref, others_ref = refs[-7:-5]
    count = len(order)
    context_refs = refs[: count + 1]
    slots, _, tile = held.shape
    depth = w_out_ref.shape[0]
    steps = out_ref.shape[1] // tile

    def copies(step, slot):
        at = pl.ds(pl.multiple_of(step * tile, tile), tile)
        sources = [w_out_ref.at[:, at]] + [others_ref.at[index, :, at] for index in order]
        return [
            pltpu.make_async_copy(
                source, held.at[slot, pl.ds(i * depth, depth)], sems.at[slot, i]
            )
            for i, source in enumerate(sources)
        ]

    gathers = [
        pltpu.make_async_copy(
            ref, stacked.at[:, pl.ds(i * depth, depth)], context_sems.at[i]
        )
        for i, ref in enumerate(context_refs)
    ]
    for gather in gathers:
        gather.start()
    for step in range(slots - 1):
        for copy in copies(step, step):
            copy.start()
    for gather in gathers:
        gather.wait()

    def one(step, carry):
        slot = lax.rem(step, slots)
        for copy in copies(step, slot):
            copy.wait()

        @pl.when(step + slots - 1 < steps)
        def _():
            for copy in copies(step + slots - 1, lax.rem(step + slots - 1, slots)):
                copy.start()

        total = jnp.dot(stacked[...], held[slot], preferred_element_type=jnp.float32)
        out_ref[:, pl.ds(pl.multiple_of(step * tile, tile), tile)] = total.astype(out_ref.dtype)
        return carry

    lax.fori_loop(0, steps, one, 0)


def out_terms(contexts, order, w_out, others):
    rows, depth = contexts[0].shape
    width = w_out.shape[1]
    tile, slots, count = 512, 3, len(contexts)
    anywhere = pl.BlockSpec(memory_space=pl.ANY)
    return pl.pallas_call(
        functools.partial(out_kernel, order),
        grid=(1,),
        in_specs=[anywhere] * (count + 2),
        out_specs=whole((rows, width)),
        out_shape=jax.ShapeDtypeStruct((rows, width), jnp.bfloat16),
        scratch_shapes=[
            pltpu.VMEM((rows, count * depth), jnp.bfloat16),
            pltpu.VMEM((slots, count * depth, tile), jnp.bfloat16),
            pltpu.SemaphoreType.DMA((slots, count)),
            pltpu.SemaphoreType.DMA((count,)),
        ],
        compiler_params=pltpu.CompilerParams(vmem_limit_bytes=VMEM_LIMIT),
        cost_estimate=pl.CostEstimate(
            flops=2 * count * rows * depth * width,
            bytes_accessed=2 * count * depth * width,
            transcendentals=0,
        ),
        name="out_terms",
    )(*contexts, w_out, others)


def reorder_kernel(source_ref, in_ref, out_ref):
    def one(i, carry):
        out_ref[i] = in_ref[source_ref[i]]
        return carry

    lax.fori_loop(0, in_ref.shape[0], one, 0)


def routed(pieces, source):
    scattered = lax.all_to_all(pieces, "dp", 0, 0, tiled=False)
    ordered = pl.pallas_call(
        reorder_kernel,
        grid=(1,),
        in_specs=[pl.BlockSpec(memory_space=pltpu.SMEM), whole(pieces.shape)],
        out_specs=whole(pieces.shape),
        out_shape=jax.ShapeDtypeStruct(pieces.shape, pieces.dtype),
        name="reorder",
    )(source, scattered)
    return lax.all_to_all(ordered, "dp", 0, 0, tiled=False)


def assemble_kernel(spots, place_ref, pieces_ref, out_ref):
    quarters = len(spots) // 2
    rows = out_ref.shape[0] // quarters
    half = rows // 2
    for quarter in range(quarters):
        base = pl.multiple_of(lax.rem(place_ref[0] + quarter, quarters) * rows, rows)
        for which in (0, 1):
            slot, at = spots[2 * quarter + which]
            for kind in range(2):
                block = pieces_ref[
                    kind * 16 + at // 16 : kind * 16 + (at + half) // 16,
                    slot * 16 : (slot + 1) * 16,
                ].reshape(half, 2 * HD)
                for head in range(2):
                    to = (2 * head + kind) * HD
                    out_ref[pl.ds(base + which * half, half), to : to + HD] = block[
                        :, head * HD : (head + 1) * HD
                    ]


def assemble(spots, place, pieces, shape):
    return pl.pallas_call(
        functools.partial(assemble_kernel, spots),
        grid=(1,),
        in_specs=[pl.BlockSpec(memory_space=pltpu.SMEM), whole(pieces.shape)],
        out_specs=whole(shape),
        out_shape=jax.ShapeDtypeStruct(shape, pieces.dtype),
        compiler_params=pltpu.CompilerParams(vmem_limit_bytes=16 << 20),
        name="assemble",
    )(jnp.reshape(place, (1,)).astype(jnp.int32), pieces)


def shards(tokens, doc_ids, destinations, norm_gain, w_query, w_key, w_value, w_out):
    quarters = lax.axis_size("ctx")
    groups = lax.axis_size("dp")
    place = lax.axis_index("ctx")
    row = lax.axis_index("dp")
    rows = tokens.shape[1]
    half = rows // 2

    ids = [doc_ids[0]] + [shifted(doc_ids[0], "ctx", -e) for e in range(1, quarters)]

    share = w_out.shape[0] // groups
    mine = lax.dynamic_slice_in_dim(w_out, row * share, share, 0)
    shares = jnp.stack([shifted(mine, "ctx", e) for e in range(1, quarters)])

    normed = normalised(tokens[0], norm_gain)
    low, high = normed[:half], normed[half:]
    shares, ids, _ = lax.optimization_barrier((shares, ids, (low, high)))
    others = lax.all_gather(shares, "dp", axis=1, tiled=True)
    before_low, after_high = shifted(low, "ctx", 1), shifted(high, "ctx", -1)
    halves = [tuple((q, h) for h in (0, 1)) for q in (0, 1, 3, 2)]
    where = {h: (i, j * half) for i, pair in enumerate(halves) for j, h in enumerate(pair)}

    bases = [(place + e) % quarters * rows for e in range(quarters)]
    steps = jnp.arange(half, dtype=jnp.int32)
    order = [h for pair in halves for h in pair]
    row_index = jnp.concatenate([bases[q] + (h * half + steps) for q, h in order])
    row_ids = jnp.concatenate([ids[q][h * half : (h + 1) * half] for q, h in order])
    first = jnp.min(
        jnp.where(row_ids[:, None] == row_ids[None, :], row_index[None, :], quarters * rows), axis=-1
    )
    cosine, sine = rotary_tables((row_index - first).astype(jnp.float32))
    first_wide = jnp.broadcast_to(first[:, None], (first.shape[0], HD))
    infos = []
    for e in range(quarters):
        lot, at = where[(e, 0)]
        least = first[lot * rows + at]
        count = 1 + (least < bases[e]).astype(jnp.int32) + (least < bases[e] - rows).astype(jnp.int32)
        infos.append(jnp.stack([count, bases[e]]))
    anchors = jnp.arange(groups, dtype=jnp.int32)
    source = jnp.sum(jnp.where(destinations[None, :] == anchors[:, None], anchors[None, :], 0), axis=1)
    cosine, sine, first_wide, infos, source = lax.optimization_barrier(
        (cosine, sine, first_wide, infos, source)
    )

    plan = [
        (
            [where[(q % quarters, h)] for q in (e - 2, e - 1, e) for h in (0, 1)],
            [where[(e, h)] for h in (0, 1)],
        )
        for e in range(quarters)
    ]
    weights = (w_query, w_key, w_value)
    tables = (cosine, sine)
    then_low, then_high, _ = lax.optimization_barrier((low, high, first))
    before_high, after_low = shifted(then_high, "ctx", 1), shifted(then_low, "ctx", -1)
    (own,) = project("all", 0, (low, high), tables, weights)
    before_low, after_high, own = lax.optimization_barrier((before_low, after_high, own))
    far = (shifted(before_low, "ctx", 1), shifted(after_high, "ctx", -1))
    arrived = (after_low, after_high, before_low, before_high)
    (near,) = project("all", rows, arrived, tables, weights)
    (next_one,) = attend([infos[1]], first_wide, (own, near, own), [(near, 0, 1)], [plan[1]])
    *far, next_one = lax.optimization_barrier((*far, next_one))
    far_kv, pieces = project("kv", 3 * rows, far, tables, weights, (own, near))
    kv = (own, near, far_kv)
    (opposite,) = project(
        "q", 3 * rows, far, tables, weights, kv, (infos[2], first_wide, plan[2])
    )
    (previous,) = attend([infos[3]], first_wide, kv, [(near, 1, 2)], [plan[3]])
    received = [shifted(c, "ctx", e) for c, e in ((opposite, 2), (next_one, 1), (previous, 3))]

    delivered = routed(pieces, source)
    (mine_context,) = attend([infos[0]], first_wide, kv, [(own, 0, 0)], [plan[0]])
    attended = out_terms([mine_context, *received], (1, 0, 2), w_out, others)
    delivered, attended = lax.optimization_barrier((delivered, attended))
    spots = tuple(where[(q, h)] for q in range(quarters) for h in (0, 1))
    shape = (quarters * rows, w_key.shape[1] + w_value.shape[1])
    kv_cache = assemble(spots, place, delivered, shape)
    return attended[None], kv_cache[None]


def solution(mesh):
    return jax.shard_map(
        shards,
        mesh=mesh,
        in_specs=(
            P("dp", "ctx", None),
            P("dp", "ctx"),
            P(),
            P(),
            P(None, "ctx"),
            P(None, "ctx"),
            P(None, "ctx"),
            P("ctx", None),
        ),
        out_specs=(P("dp", "ctx", None), P("dp", None, "ctx")),
        check_vma=False,
    )
```
